512 devices in a mesh: row: 8 (over x_lo, y), col: 64 (over z, x_hi, core).
Axes of the slice: x: 4 (x_hi: 2, x_lo: 2; x = x_hi * 2 + x_lo), y: 4, z: 16, core: 2. Of those that a mesh axis runs over, the one named last changes fastest.
Arguments:
- tiles: bfloat16 [512, 384, 512], P('row', 'col')
- block_cols: int32 [8, 384], P('row', 'col'), may hold values from 0 to 7, as said below
- signs: int32 [262144], P('col'), may hold values from -1 to 1, as said below
- samples: int32 [4096], replicated, may hold values from 0 to 262143, as said below
Outputs:
- sketch: float32 [512, 4096], P('row', 'col')
- gram: float32 [4096, 4096], P('row', 'col')
The draws below stay inside these ranges and needn't reach their ends.
Inputs may be any that keep to these rules, and one draw needn't show every extreme that they name: `signs`: every entry is -1 or +1. The 6 entries block_cols[r, c * 6 + t], t < 6, of one row slab r and column slab c are distinct. `samples`: entry k lies in column slab k // 64, that is from (k // 64) * 4096 to (k // 64 + 1) * 4096 - 1; the 64 entries of one slab are distinct.
All inputs are finite; a program needn't handle non-finite values.
Results may differ from the reference program's by a relative error of at most 0.004.
Values may be sent and summed in bfloat16 or wider, within the bound.
A program may use at most 64 MiB of HBM per device.

```python
import math
import jax
import jax.numpy as jnp
from jax import lax

N = 262144
TW = 512
K = 4096
TILES_DEV = 6
ROWS_DEV = 64
M = 512
RSLABS = 8
SLAB = 4096
NB = 8
KD = 64
NT = 384


def draw_signs(key, part):
    key = jax.random.fold_in(key, 11)
    return (jax.random.randint(key, (N,), 0, 2) * 2 - 1).astype(jnp.int32)


def draw_samples(key, part):
    key = jax.random.fold_in(key, 12)
    ncol = N // SLAB
    keys = jax.random.split(key, ncol)

    def pick(sub):
        first, second = jax.random.split(sub)
        inner = (jax.random.permutation(first, SLAB - 2)[:KD - 2] + 1).astype(jnp.int32)
        ends = jnp.array([0, SLAB - 1], dtype=jnp.int32)
        chosen = jnp.concatenate([ends, inner])
        return jax.random.permutation(second, chosen)
    lows = jax.vmap(pick)(keys)
    starts = (jnp.arange(ncol, dtype=jnp.int32) * SLAB)[:, None]
    return (lows.astype(jnp.int32) + starts).reshape(K).astype(jnp.int32)


def draw_block_cols(key, part):
    key = jax.random.fold_in(key, 13)
    ncol = N // SLAB
    keys = jax.random.split(key, RSLABS * ncol)

    def pick(sub):
        return jax.random.permutation(sub, NB)[:TILES_DEV]
    chosen = jax.vmap(pick)(keys)
    return chosen.reshape(RSLABS, NT).astype(jnp.int32)


def draw_tiles(key, part):
    key = jax.random.fold_in(key, 14)
    first, second = jax.random.split(key, 2)
    sigma = math.sqrt(K / (NT * TW))
    base = jax.random.normal(first, (M, NT, TW), jnp.float32)
    scales = jnp.exp(jax.random.uniform(second, (M, 1, 1), jnp.float32, math.log(0.3), math.log(3.0)))
    return (base * scales * sigma).astype(jnp.bfloat16)


def setup_inputs(seed: int = 0) -> dict:
    seeds = jax.random.split(jax.random.key(seed), 5)
    return {
        "tiles": draw_tiles(jax.random.fold_in(seeds[4], 71), 0),
        "block_cols": draw_block_cols(jax.random.fold_in(seeds[4], 71), 0),
        "signs": draw_signs(jax.random.fold_in(seeds[4], 71), 0),
        "samples": draw_samples(jax.random.fold_in(seeds[4], 71), 0),
    }


def parity(value, bits):
    result = jnp.zeros_like(value)
    for shift in range(bits):
        result = result ^ value >> shift & 1
    return result

def hadamard(left, right, bits):
    return (1 - 2 * parity(left & right, bits)).astype(jnp.float32)

def reference(tiles, block_cols, signs, samples):
    ncol = N // SLAB
    tw_bits = (TW - 1).bit_length()
    nb_bits = (NB - 1).bit_length()
    col_bits = (ncol - 1).bit_length()
    blocks = tiles.reshape(RSLABS, ROWS_DEV, ncol, TILES_DEV, TW)
    columns = block_cols.reshape(RSLABS, ncol, TILES_DEV)
    sign_blocks = signs.reshape(ncol, NB, TW)
    lows = jnp.arange(TW, dtype=jnp.int32)
    h_small = hadamard(lows[:, None], lows[None, :], tw_bits)
    block_ids = jnp.arange(NB, dtype=jnp.int32)
    slab_of = samples // SLAB
    local = samples - slab_of * SLAB

    def one_slab(total, slab_index):
        tile_c = lax.dynamic_index_in_dim(blocks, slab_index, 2, keepdims=False)
        col_c = lax.dynamic_index_in_dim(columns, slab_index, 1, keepdims=False)
        sign_c = lax.dynamic_index_in_dim(sign_blocks, slab_index, 0, keepdims=False)
        picked = sign_c[col_c].astype(jnp.float32)
        signed = tile_c.astype(jnp.float32) * picked[:, None, :, :]
        product = jnp.einsum('rmtl,lj->rmtj', signed, h_small, precision=lax.Precision.HIGHEST)
        coef = hadamard(col_c[:, :, None], block_ids[None, None, :], nb_bits)
        field = jnp.einsum('rth,rmtj->rmhj', coef, product, precision=lax.Precision.HIGHEST)
        field = field.reshape(M, SLAB)
        outer = hadamard(slab_index, slab_of, col_bits)
        return (total + jnp.take(field, local, axis=1) * outer[None, :], None)
    total, _ = lax.scan(one_slab, jnp.zeros((M, K), jnp.float32), jnp.arange(ncol, dtype=jnp.int32))
    sketch = total * (1.0 / math.sqrt(K))
    rounded = sketch.astype(jnp.bfloat16)
    gram = jnp.dot(rounded.T, rounded, preferred_element_type=jnp.float32) / M
    return (sketch, gram)
```

```python
import functools
import math

import jax
import jax.numpy as jnp
from jax import lax
from jax.experimental import pallas as pl
from jax.experimental.pallas import tpu as pltpu
from jax.sharding import PartitionSpec as P

MESH = pl.DeviceIdType.MESH
QUAD = 4
LANES = 128
F32 = jnp.float32
BF16 = jnp.bfloat16


def parity_sign(bits):
    for shift in (8, 4, 2, 1):
        bits = bits ^ (bits >> shift)
    return (1 - 2 * (bits & 1)).astype(F32)


def alternating(k):
    return ((k + 1) // 2) * (1 - 2 * (k % 2))


def remote(src, dst, send_sem, recv_sem, device):
    return pltpu.make_async_remote_copy(
        src_ref=src,
        dst_ref=dst,
        send_sem=send_sem,
        recv_sem=recv_sem,
        device_id=device,
        device_id_type=MESH,
    )


def wait_bytes(ref, sem):
    pltpu.make_async_copy(ref, ref, sem).wait()


def kernel(
    nrow,
    nz,
    tiles_hbm,
    block_ref,
    signs_ref,
    samples_ref,
    sketch_ref,
    gram_ref,
    tl,
    xs,
    xr,
    bs,
    br,
    hop,
    acc,
    csend,
    crecv,
    ag,
    sbx,
    skx,
    sk,
    sc,
    sr,
    tile_sem,
    a_send,
    a_recv,
    b_send,
    b_recv,
    c_send,
    c_recv,
    g_send,
    g_recv,
    k_send,
    k_recv,
    s_send,
    s_recv,
    f_send,
    f_recv,
):
    slots, rows, tile_width = tl.shape
    part = rows // QUAD
    width = samples_ref.shape[0] * LANES
    plane_cols = width // nz
    planes = nz // nrow
    chunk = planes * plane_cols
    nchunk = width // chunk
    plane_devs = nrow * QUAD
    row = lax.axis_index("row")
    col = lax.axis_index("col")
    z = col // QUAD
    q = col % QUAD
    mine = row * QUAD + q
    my_chunk = z // planes

    def z_peer(offset):
        return (z + offset) % nz

    def plane_peer(offset):
        other = (mine + offset) % plane_devs
        return other // QUAD, other % QUAD

    def far_first(k):
        return nz // 2 + alternating(k)

    barrier = pltpu.get_barrier_semaphore()

    def greet_z(k, _):
        pl.semaphore_signal(
            barrier, inc=1, device_id=(row, z_peer(far_first(k)) * QUAD + q), device_id_type=MESH
        )
        return 0

    def greet_plane(k, _):
        r2, q2 = plane_peer(k)
        pl.semaphore_signal(barrier, inc=1, device_id=(r2, z * QUAD + q2), device_id_type=MESH)
        return 0

    lax.fori_loop(0, nz - 1, greet_z, 0)
    lax.fori_loop(1, plane_devs, greet_plane, 0)

    fetch = pltpu.make_async_copy(tiles_hbm, tl, tile_sem)
    fetch.start()

    low_bits = (tile_width - 1).bit_length()

    def fill(blk, _):
        low = samples_ref[pl.ds(blk, 1), :] & (tile_width - 1)
        lanes = pl.ds(pl.multiple_of(blk * LANES, LANES), LANES)
        base = parity_sign(lax.broadcasted_iota(jnp.int32, (16, LANES), 0) & low).astype(BF16)
        group = [base]
        for bit in range(4, low_bits):
            sign = (1 - 2 * ((low >> bit) & 1)).astype(F32)
            sign = jnp.broadcast_to(sign, (16, LANES)).astype(BF16)
            group = group + [g * sign for g in group]
        for i, g in enumerate(group):
            hop[16 * i : 16 * i + 16, lanes] = g
        return 0

    lax.fori_loop(0, width // LANES, fill, 0)

    fetch.wait()
    per_block = tile_width // LANES
    where_row = lax.broadcasted_iota(jnp.int32, (8, LANES), 0)
    codes = jnp.zeros((8, LANES), jnp.int32)
    for t in range(slots):
        block = block_ref[0, t]
        codes = jnp.where(where_row == t, col * (signs_ref.shape[0] // per_block) + block, codes)
        for j in range(per_block):
            sign = signs_ref[pl.ds(block * per_block + j, 1), :].astype(F32)
            sign = jnp.broadcast_to(sign, (part, LANES)).astype(BF16)
            cut = slice(j * LANES, (j + 1) * LANES)
            for p in range(QUAD):
                xs[p, t * part : (t + 1) * part, cut] = tl[t, p * part : (p + 1) * part, cut] * sign
    bs[...] = codes

    pl.semaphore_wait(barrier, nz - 1 + plane_devs - 1)

    for o in (2, 3, 1):
        q2 = q ^ o
        device = (row, z * QUAD + q2)
        remote(bs, br.at[o - 1], b_send.at[0], b_recv.at[o - 1], device).start()
        remote(xs.at[q2], xr.at[o - 1], a_send.at[0], a_recv.at[o - 1], device).start()

    def terms(ch, first, sources):
        cols = pl.ds(pl.multiple_of(ch * chunk, chunk), chunk)
        operator = hop[:, cols]
        sums = [None] * (chunk // LANES)
        for x, code in sources:
            y = jnp.dot(x, operator, preferred_element_type=F32)
            for i in range(chunk // LANES):
                high = samples_ref[pl.ds(ch * (chunk // LANES) + i, 1), :] >> low_bits
                coef = parity_sign(code & high)
                for t in range(slots):
                    term = y[t * part : (t + 1) * part, i * LANES : (i + 1) * LANES] * coef[t : t + 1, :]
                    sums[i] = term if sums[i] is None else sums[i] + term
        total = jnp.concatenate(sums, axis=1)
        if not first:
            total = total + acc[:, cols]
        acc[:, cols] = total
        return total

    def own_terms(ch, _):
        terms(ch, True, [(xs[q], bs[...])])
        return 0

    lax.fori_loop(0, nchunk, own_terms, 0)

    def received(o):
        wait_bytes(br.at[o - 1], b_recv.at[o - 1])
        wait_bytes(xr.at[o - 1], a_recv.at[o - 1])

    received(1)

    def sibling_terms(ch, _):
        terms(ch, False, [(xr[0], br[0])])
        return 0

    lax.fori_loop(0, nchunk, sibling_terms, 0)
    received(2)
    received(3)

    def last_terms(k, _):
        ch = (my_chunk + nchunk // 2 + alternating(k) + nchunk) % nchunk
        total = terms(ch, False, [(xr[1], br[1]), (xr[2], br[2])])
        for i in range(planes):
            z2 = ch * planes + i
            csend[z2] = total[:, i * plane_cols : (i + 1) * plane_cols].astype(BF16)

            @pl.when(z2 != z)
            def _():
                slot = (z - z2 + nz) % nz - 1
                remote(
                    csend.at[z2], crecv.at[slot], c_send.at[0], c_recv.at[0], (row, z2 * QUAD + q)
                ).start()

        return 0

    lax.fori_loop(0, nchunk, last_terms, 0)

    wait_bytes(crecv, c_recv.at[0])
    total = acc[:, pl.ds(pl.multiple_of(z * plane_cols, plane_cols), plane_cols)]
    for i in range(nz - 1):
        total = total + crecv[i].astype(F32)
    total = total * (1.0 / math.sqrt(width))
    rounded = total.astype(BF16)
    ag[z] = rounded
    half = plane_cols // 2
    for i in range(2):
        sbx[i] = rounded[:, i * half : (i + 1) * half]
        skx[i] = total[:, i * half : (i + 1) * half]

    def spread(k, _):
        z2 = z_peer(far_first(k))
        remote(ag.at[z], ag.at[z], g_send.at[0], g_recv.at[z], (row, z2 * QUAD + q)).start()
        return 0

    lax.fori_loop(0, nz - 1, spread, 0)

    my_part = pl.ds(pl.multiple_of(q * part, part), part)
    my_rows = pl.ds(pl.multiple_of(row * rows + q * part, part), part)
    for o in (2, 3, 1):
        q2 = q ^ o
        remote(skx.at[q2 // 2], sk.at[my_part], k_send.at[0], k_recv.at[0], (row, z * QUAD + q2)).start()
    pltpu.make_async_copy(skx.at[q // 2], sk.at[my_part], k_recv.at[0]).start()

    def in_plane(k, _):
        r2, q2 = plane_peer(k)
        remote(sbx.at[q2 // 2], sc.at[my_rows], s_send.at[0], s_recv.at[0], (r2, z * QUAD + q2)).start()
        return 0

    lax.fori_loop(1, plane_devs, in_plane, 0)
    pltpu.make_async_copy(sbx.at[q // 2], sc.at[my_rows], s_recv.at[0]).start()

    def forward(k, _):
        p = (my_chunk + alternating(k) + nrow) % nrow
        first = p * planes

        def arrived(i, _):
            z2 = first + i

            @pl.when(z2 != z)
            def _():
                wait_bytes(ag.at[z2], g_recv.at[z2])

            return 0

        lax.fori_loop(0, planes, arrived, 0)

        def send(i, _):
            q2 = (q + i) % QUAD
            here = jnp.logical_and(p == row, i == 0)
            src = ag.at[pl.ds(first, planes)]

            @pl.when(here)
            def _():
                pltpu.make_async_copy(src, sr.at[:, my_rows], f_recv.at[0]).start()

            @pl.when(jnp.logical_not(here))
            def _():
                remote(src, sr.at[:, my_rows], f_send.at[0], f_recv.at[0], (p, z * QUAD + q2)).start()

            return 0

        lax.fori_loop(0, QUAD, send, 0)
        return 0

    lax.fori_loop(0, nrow, forward, 0)

    odd = q % 2
    wait_bytes(sk, k_recv.at[0])
    mine_cols = half // 2
    sketch_ref[...] = jnp.where(odd == 0, sk[:, :mine_cols], sk[:, mine_cols:])
    wait_bytes(sc, s_recv.at[0])
    right = sc[...]
    wait_bytes(sr, f_recv.at[0])
    for i in range(planes):
        product = lax.dot_general(
            right, sr[i], (((0,), (0,)), ((), ())), preferred_element_type=F32
        )
        product = jnp.where(odd == 0, product[:mine_cols], product[mine_cols:])
        gram_ref[:, i * plane_cols : (i + 1) * plane_cols] = product * (1.0 / (rows * nrow))

    wait_bytes(br, b_send.at[0])
    wait_bytes(xr, a_send.at[0])
    wait_bytes(crecv, c_send.at[0])
    wait_bytes(ag.at[pl.ds(0, nz - 1)], g_send.at[0])
    wait_bytes(sk.at[pl.ds(0, rows - part)], k_send.at[0])
    wait_bytes(sc.at[pl.ds(0, rows * nrow - part)], s_send.at[0])
    wait_bytes(sr.at[:, pl.ds(0, rows * nrow - part)], f_send.at[0])


def per_device(nrow, nz, tiles, block_cols, signs, samples):
    rows, slots, tile_width = tiles.shape
    width = samples.shape[0]
    part = rows // QUAD
    plane_cols = width // nz
    planes = nz // nrow
    own = plane_cols // QUAD
    dma = pltpu.SemaphoreType.DMA
    vmem = pl.BlockSpec(memory_space=pltpu.VMEM)
    sketch, gram_t = pl.pallas_call(
        functools.partial(kernel, nrow, nz),
        out_shape=(
            jax.ShapeDtypeStruct((rows, own), F32),
            jax.ShapeDtypeStruct((own, planes * plane_cols), F32),
        ),
        in_specs=[
            pl.BlockSpec(memory_space=pl.ANY),
            pl.BlockSpec(memory_space=pltpu.SMEM),
            vmem,
            vmem,
        ],
        out_specs=(vmem, vmem),
        scratch_shapes=[
            pltpu.VMEM((slots, rows, tile_width), BF16),
            pltpu.VMEM((QUAD, slots * part, tile_width), BF16),
            pltpu.VMEM((QUAD - 1, slots * part, tile_width), BF16),
            pltpu.VMEM((8, LANES), jnp.int32),
            pltpu.VMEM((QUAD - 1, 8, LANES), jnp.int32),
            pltpu.VMEM((tile_width, width), BF16),
            pltpu.VMEM((part, width), F32),
            pltpu.VMEM((nz, part, plane_cols), BF16),
            pltpu.VMEM((nz - 1, part, plane_cols), BF16),
            pltpu.VMEM((nz, part, plane_cols), BF16),
            pltpu.VMEM((2, part, plane_cols // 2), BF16),
            pltpu.VMEM((2, part, plane_cols // 2), F32),
            pltpu.VMEM((rows, plane_cols // 2), F32),
            pltpu.VMEM((rows * nrow, plane_cols // 2), BF16),
            pltpu.VMEM((planes, rows * nrow, plane_cols), BF16),
            dma,
            dma((1,)),
            dma((QUAD - 1,)),
            dma((1,)),
            dma((QUAD - 1,)),
            dma((1,)),
            dma((1,)),
            dma((1,)),
            dma((nz,)),
            dma((1,)),
            dma((1,)),
            dma((1,)),
            dma((1,)),
            dma((1,)),
            dma((1,)),
        ],
        compiler_params=pltpu.CompilerParams(
            collective_id=0, has_side_effects=True, vmem_limit_bytes=32 << 20
        ),
    )(
        tiles.transpose(1, 0, 2),
        block_cols,
        signs.reshape(-1, LANES),
        samples.reshape(-1, LANES),
    )
    return sketch, gram_t.T


def solution(mesh):
    nrow = mesh.shape["row"]
    nz = mesh.shape["col"] // QUAD
    return jax.shard_map(
        functools.partial(per_device, nrow, nz),
        mesh=mesh,
        in_specs=(P("row", "col", None), P("row", "col"), P("col"), P()),
        out_specs=(P("row", "col"), P("row", "col")),
        check_vma=False,
    )
```

```python
import functools
import math

import jax
import jax.numpy as jnp
from jax import lax
from jax.experimental import pallas as pl
from jax.experimental.pallas import tpu as pltpu
from jax.sharding import PartitionSpec as P

MESH = pl.DeviceIdType.MESH
CHIPS = 2
CORES = 2
QUAD = CHIPS * CORES
LANES = 128
F32 = jnp.float32
BF16 = jnp.bfloat16


def parity_sign(bits):
    for shift in (8, 4, 2, 1):
        bits = bits ^ (bits >> shift)
    return (1 - 2 * (bits & 1)).astype(F32)


def alternating(k):
    return lax.div(k + 1, 2) * (1 - 2 * lax.rem(k, 2))


def remote(src, dst, send_sem, recv_sem, device):
    return pltpu.make_async_remote_copy(
        src_ref=src,
        dst_ref=dst,
        send_sem=send_sem,
        recv_sem=recv_sem,
        device_id=device,
        device_id_type=MESH,
    )


def wait_bytes(ref, sem):
    pltpu.make_async_copy(ref, ref, sem).wait()


def kernel(
    nrow,
    nz,
    tiles_hbm,
    block_hbm,
    signs_hbm,
    samples_hbm,
    sketch_ref,
    gram_ref,
    tl,
    blocks,
    signs,
    samples,
    xs,
    hop,
    terms,
    terms2,
    halves,
    other,
    other2,
    own,
    csend,
    crecv,
    ag,
    sk,
    sc,
    sr,
    gs,
    gr,
    in_sem,
    a_send,
    a_recv,
    x_send,
    x_recv,
    c_send,
    c_recv,
    g_send,
    g_recv,
    k_send,
    k_recv,
    s_send,
    s_recv,
    f_send,
    f_recv,
    o_send,
    o_recv,
):
    slots, rows, tile_width = tl.shape
    part = rows // CORES
    width = samples.shape[0] * LANES
    planes = nz // nrow
    chunk = planes * CHIPS * LANES
    nchunk = width // chunk
    row = lax.axis_index("row")
    col = lax.axis_index("col")
    z = lax.div(col, QUAD)
    q = lax.rem(col, QUAD)
    h = lax.div(q, CORES)
    core = lax.rem(q, CORES)
    my_chunk = lax.div(z, planes)
    sibling = (row, col + 1 - 2 * core)
    partner = (row, col + CORES * (1 - 2 * h))

    def at(z2, h2, core2):
        return z2 * QUAD + h2 * CORES + core2

    def far_first(k):
        return nz // 2 + alternating(k)

    fetches = [
        pltpu.make_async_copy(src, dst, in_sem.at[i])
        for i, (src, dst) in enumerate(
            [(block_hbm, blocks), (signs_hbm, signs), (tiles_hbm, tl), (samples_hbm, samples)]
        )
    ]
    for fetch in fetches:
        fetch.start()

    barrier = pltpu.get_barrier_semaphore()

    def greet_plane(k, _):
        mate = lax.rem(row * QUAD + q + k, nrow * QUAD)
        device = (lax.div(mate, QUAD), z * QUAD + lax.rem(mate, QUAD))
        pl.semaphore_signal(barrier, inc=1, device_id=device, device_id_type=MESH)
        return 0

    def greet_line(k, _):
        device = (row, at(lax.rem(z + far_first(k), nz), h, core))
        pl.semaphore_signal(barrier, inc=1, device_id=device, device_id_type=MESH)
        return 0

    lax.fori_loop(0, nz - 1, greet_line, 0)
    lax.fori_loop(1, nrow * QUAD, greet_plane, 0)

    per_block = tile_width // LANES
    where_row = lax.broadcasted_iota(jnp.int32, (8, LANES), 0)
    codes = jnp.zeros((8, LANES), jnp.int32)
    for fetch in fetches[:3]:
        fetch.wait()
    for t in range(slots):
        block = blocks[0, t]
        codes = jnp.where(where_row == t, col * (signs.shape[0] // per_block) + block, codes)
        for j in range(per_block):
            sign = signs[pl.ds(block * per_block + j, 1), :].astype(F32)
            sign = jnp.broadcast_to(sign, (rows, LANES)).astype(BF16)
            cut = slice(j * LANES, (j + 1) * LANES)
            xs[t * rows : (t + 1) * rows, cut] = tl[t, :, cut] * sign

    low_bits = (tile_width - 1).bit_length()
    fetches[3].wait()

    def fill(blk, _):
        low = samples[pl.ds(blk, 1), :] & (tile_width - 1)
        lanes = pl.ds(pl.multiple_of(blk * LANES, LANES), LANES)
        base = parity_sign(lax.broadcasted_iota(jnp.int32, (16, LANES), 0) & low).astype(BF16)
        group = [base]
        for bit in range(4, low_bits):
            sign = (1 - 2 * ((low >> bit) & 1)).astype(F32)
            sign = jnp.broadcast_to(sign, (16, LANES)).astype(BF16)
            group = group + [g * sign for g in group]
        for i, g in enumerate(group):
            hop[16 * i : 16 * i + 16, lanes] = g
        return 0

    lax.fori_loop(0, width // LANES, fill, 0)

    def chunk_of(k):
        return lax.rem(my_chunk + nchunk // 2 + alternating(k) + nchunk, nchunk)

    def multiply(k, _):
        ch = chunk_of(k)
        operator = hop[:, pl.ds(pl.multiple_of(ch * chunk, chunk), chunk)]
        y = jnp.dot(xs[...], operator, preferred_element_type=F32)
        for i in range(chunk // LANES):
            high = samples[pl.ds(ch * (chunk // LANES) + i, 1), :] >> low_bits
            coef = parity_sign(codes & high)
            total = None
            for t in range(slots):
                term = y[t * rows : (t + 1) * rows, i * LANES : (i + 1) * LANES] * coef[t : t + 1, :]
                total = term if total is None else total + term
            for p in range(CORES):
                terms[k, p, :, i * LANES : (i + 1) * LANES] = total[p * part : (p + 1) * part]
        return 0

    lax.fori_loop(0, nchunk, multiply, 0)

    pl.semaphore_wait(barrier, nz - 1 + nrow * QUAD - 1)

    def to_sibling(k, _):
        remote(terms.at[k, 1 - core], terms2.at[k], a_send, a_recv.at[k], sibling).start()
        return 0

    lax.fori_loop(0, nchunk, to_sibling, 0)

    def to_partner(k, _):
        wait_bytes(terms2.at[k], a_recv.at[k])
        total = terms[k, core] + terms2[k]
        for i in range(planes):
            left = total[:, 2 * i * LANES : (2 * i + 1) * LANES]
            right = total[:, (2 * i + 1) * LANES : (2 * i + 2) * LANES]
            halves[k, i] = jnp.where(h == 0, left, right)
            other[k, i] = jnp.where(h == 0, right, left)
        remote(other.at[k], other2.at[k], x_send, x_recv.at[k], partner).start()
        return 0

    lax.fori_loop(0, nchunk, to_partner, 0)

    def to_planes(k, _):
        wait_bytes(other2.at[k], x_recv.at[k])
        for i in range(planes):
            z2 = chunk_of(k) * planes + i
            total = halves[k, i] + other2[k, i]

            @pl.when(z2 == z)
            def _():
                own[...] = total

            @pl.when(z2 != z)
            def _():
                csend[z2] = total.astype(BF16)
                slot = lax.rem(z - z2 + nz, nz) - 1
                remote(csend.at[z2], crecv.at[slot], c_send, c_recv, (row, at(z2, h, core))).start()

        return 0

    lax.fori_loop(0, nchunk, to_planes, 0)

    wait_bytes(crecv, c_recv)
    total = own[...]
    for i in range(nz - 1):
        total = total + crecv[i].astype(F32)
    total = total * (1.0 / math.sqrt(width))
    ag[z] = total.astype(BF16)

    def spread(k, _):
        device = (row, at(lax.rem(z + far_first(k), nz), h, core))
        remote(ag.at[z], ag.at[z], g_send, g_recv.at[z], device).start()
        return 0

    lax.fori_loop(0, nz - 1, spread, 0)

    my_rows = pl.ds(pl.multiple_of(row * rows + core * part, part), part)

    def in_plane(k, _):
        mate = lax.rem(row * CORES + core + k, nrow * CORES)
        device = (lax.div(mate, CORES), at(z, h, lax.rem(mate, CORES)))
        remote(ag.at[z], sc.at[my_rows], s_send, s_recv, device).start()
        return 0

    lax.fori_loop(1, nrow * CORES, in_plane, 0)
    pltpu.make_async_copy(ag.at[z], sc.at[my_rows], s_recv).start()

    sk[0] = total
    swap_sketch = remote(sk.at[0], sk.at[1], k_send, k_recv, sibling)
    swap_sketch.start()

    my_cols = pl.ds(pl.multiple_of(h * LANES, LANES), LANES)

    def forward(k, _):
        p = lax.rem(my_chunk + alternating(k) + nrow, nrow)
        for i in range(planes):
            z2 = p * planes + i

            @pl.when(z2 != z)
            def _():
                wait_bytes(ag.at[z2], g_recv.at[z2])

            for h2 in range(CHIPS):
                here = jnp.logical_and(p == row, jnp.logical_and(h2 == h, i == core))

                @pl.when(here)
                def _():
                    pltpu.make_async_copy(ag.at[z2], sr.at[my_rows, my_cols], f_recv).start()

                @pl.when(jnp.logical_not(here))
                def _():
                    remote(
                        ag.at[z2], sr.at[my_rows, my_cols], f_send, f_recv, (p, at(z, h2, i))
                    ).start()

        return 0

    lax.fori_loop(0, nrow, forward, 0)

    half = LANES // CORES
    swap_sketch.wait()
    for i in range(CORES):
        block = sk[jnp.where(core == i, 0, 1)]
        sketch_ref[i * part : (i + 1) * part, :] = jnp.where(core == 0, block[:, :half], block[:, half:])

    wait_bytes(sc, s_recv)
    wait_bytes(sr, f_recv)
    product = lax.dot_general(
        sc[...], sr[...], (((0,), (0,)), ((), ())), preferred_element_type=F32
    ) * (1.0 / (rows * nrow))
    gs[...] = jnp.where(core == 0, product[half:], product[:half])
    swap_product = remote(gs, gr, o_send, o_recv, sibling)
    swap_product.start()
    mine = jnp.where(core == 0, product[:half], product[half:])
    swap_product.wait()
    theirs = gr[...]
    cols = CHIPS * LANES
    gram_ref[:, :cols] = jnp.where(core == 0, mine, theirs)
    gram_ref[:, cols:] = jnp.where(core == 0, theirs, mine)

    wait_bytes(terms2, a_send)
    wait_bytes(other2, x_send)
    wait_bytes(crecv, c_send)
    wait_bytes(crecv, g_send)
    wait_bytes(sc.at[pl.ds(0, rows * nrow - part)], s_send)
    wait_bytes(sr.at[pl.ds(0, rows * nrow - part // CHIPS)], f_send)


def per_device(nrow, nz, tiles, block_cols, signs, samples):
    rows, slots, tile_width = tiles.shape
    width = samples.shape[0]
    part = rows // CORES
    half = LANES // CORES
    planes = nz // nrow
    chunk = planes * CHIPS * LANES
    nchunk = width // chunk
    dma = pltpu.SemaphoreType.DMA
    vmem = pl.BlockSpec(memory_space=pltpu.VMEM)
    hbm = pl.BlockSpec(memory_space=pltpu.HBM)
    sketch, gram_t = pl.pallas_call(
        functools.partial(kernel, nrow, nz),
        out_shape=(
            jax.ShapeDtypeStruct((rows, half), F32),
            jax.ShapeDtypeStruct((half, width // nrow), F32),
        ),
        in_specs=[hbm, hbm, hbm, hbm],
        out_specs=(vmem, vmem),
        scratch_shapes=[
            pltpu.VMEM((slots, rows, tile_width), BF16),
            pltpu.SMEM(block_cols.shape, jnp.int32),
            pltpu.VMEM((signs.shape[0] // LANES, LANES), jnp.int32),
            pltpu.VMEM((width // LANES, LANES), jnp.int32),
            pltpu.VMEM((slots * rows, tile_width), BF16),
            pltpu.VMEM((tile_width, width), BF16),
            pltpu.VMEM((nchunk, CORES, part, chunk), F32),
            pltpu.VMEM((nchunk, part, chunk), F32),
            pltpu.VMEM((nchunk, planes, part, LANES), F32),
            pltpu.VMEM((nchunk, planes, part, LANES), F32),
            pltpu.VMEM((nchunk, planes, part, LANES), F32),
            pltpu.VMEM((part, LANES), F32),
            pltpu.VMEM((nz, part, LANES), BF16),
            pltpu.VMEM((nz - 1, part, LANES), BF16),
            pltpu.VMEM((nz, part, LANES), BF16),
            pltpu.VMEM((2, part, LANES), F32),
            pltpu.VMEM((rows * nrow, LANES), BF16),
            pltpu.VMEM((rows * nrow, CHIPS * LANES), BF16),
            pltpu.VMEM((half, CHIPS * LANES), F32),
            pltpu.VMEM((half, CHIPS * LANES), F32),
            dma((4,)),
            dma,
            dma((nchunk,)),
            dma,
            dma((nchunk,)),
            dma,
            dma,
            dma,
            dma((nz,)),
            dma,
            dma,
            dma,
            dma,
            dma,
            dma,
            dma,
            dma,
        ],
        compiler_params=pltpu.CompilerParams(
            collective_id=0, has_side_effects=True, vmem_limit_bytes=32 << 20
        ),
    )(
        *(
            pltpu.with_memory_space_constraint(x, pltpu.HBM)
            for x in (
                tiles.transpose(1, 0, 2),
                block_cols,
                signs.reshape(-1, LANES),
                samples.reshape(-1, LANES),
            )
        )
    )
    return sketch, gram_t.T


def solution(mesh):
    nrow = mesh.shape["row"]
    nz = mesh.shape["col"] // QUAD
    return jax.shard_map(
        functools.partial(per_device, nrow, nz),
        mesh=mesh,
        in_specs=(P("row", "col", None), P("row", "col"), P("col"), P()),
        out_specs=(P("row", "col"), P("row", "col")),
        check_vma=False,
    )
```

```python
import functools
import math

import jax
import jax.numpy as jnp
from jax import lax
from jax.experimental import pallas as pl
from jax.experimental.pallas import tpu as pltpu
from jax.sharding import PartitionSpec as P

MESH = pl.DeviceIdType.MESH
CHIPS = 2
CORES = 2
QUAD = CHIPS * CORES
LANES = 128
XNEAR = 4
ZNEAR = 1
F32 = jnp.float32
BF16 = jnp.bfloat16


def parity_sign(bits):
    for shift in (8, 4, 2, 1):
        bits = bits ^ (bits >> shift)
    return (1 - 2 * (bits & 1)).astype(F32)


def alternating(k):
    return lax.div(k + 1, 2) * (1 - 2 * lax.rem(k, 2))


def remote(src, dst, send_sem, recv_sem, device):
    return pltpu.make_async_remote_copy(
        src_ref=src,
        dst_ref=dst,
        send_sem=send_sem,
        recv_sem=recv_sem,
        device_id=device,
        device_id_type=MESH,
    )


def wait_bytes(ref, sem):
    pltpu.make_async_copy(ref, ref, sem).wait()


def kernel(
    nrow,
    nz,
    tiles_hbm,
    block_hbm,
    signs_hbm,
    samples_hbm,
    sketch_ref,
    gram_ref,
    tl,
    blocks,
    signs,
    samples,
    xs,
    hop0,
    hop1,
    terms,
    terms2,
    halves,
    other,
    other2,
    far,
    far2,
    own,
    csend,
    crecv,
    nsend,
    nrecv,
    ag,
    sk,
    sc,
    sr,
    gs,
    gr,
    in_sem,
    a_send,
    a_recv,
    x_send,
    y_send,
    x_recv,
    c_send,
    c_recv,
    n_send,
    n_recv,
    g_send,
    g_recv,
    k_send,
    k_recv,
    s_send,
    s_recv,
    f_send,
    f_recv,
    o_send,
    o_recv,
):
    slots, rows, tile_width = tl.shape
    part = rows // CORES
    width = samples.shape[0] * LANES
    planes = nz // nrow
    chunk = planes * CHIPS * LANES
    nchunk = width // chunk
    row = lax.axis_index("row")
    col = lax.axis_index("col")
    z = lax.div(col, QUAD)
    q = lax.rem(col, QUAD)
    h = lax.div(q, CORES)
    core = lax.rem(q, CORES)
    my_chunk = lax.div(z, planes)
    sibling = (row, col + 1 - 2 * core)
    partner = (row, col + CORES * (1 - 2 * h))

    def at(z2, h2, core2):
        return z2 * QUAD + h2 * CORES + core2

    def far_first(k):
        return nz // 2 + alternating(k)

    fetches = [
        pltpu.make_async_copy(src, dst, in_sem.at[i])
        for i, (src, dst) in enumerate(
            [(block_hbm, blocks), (signs_hbm, signs), (tiles_hbm, tl), (samples_hbm, samples)]
        )
    ]
    for fetch in fetches:
        fetch.start()

    barrier = pltpu.get_barrier_semaphore()

    def greet_plane(k, _):
        mate = lax.rem(row * QUAD + q + k, nrow * QUAD)
        device = (lax.div(mate, QUAD), z * QUAD + lax.rem(mate, QUAD))
        pl.semaphore_signal(barrier, inc=1, device_id=device, device_id_type=MESH)
        return 0

    def greet_line(k, _):
        device = (row, at(lax.rem(z + far_first(k), nz), h, core))
        pl.semaphore_signal(barrier, inc=1, device_id=device, device_id_type=MESH)
        return 0

    lax.fori_loop(0, nz - 1, greet_line, 0)
    lax.fori_loop(1, nrow * QUAD, greet_plane, 0)

    per_block = tile_width // LANES
    where_row = lax.broadcasted_iota(jnp.int32, (8, LANES), 0)
    codes = jnp.zeros((8, LANES), jnp.int32)
    for fetch in fetches[:3]:
        fetch.wait()
    for t in range(slots):
        block = blocks[0, t]
        codes = jnp.where(where_row == t, col * (signs.shape[0] // per_block) + block, codes)
        for j in range(per_block):
            sign = signs[pl.ds(block * per_block + j, 1), :].astype(F32)
            sign = jnp.broadcast_to(sign, (rows, LANES)).astype(BF16)
            cut = slice(j * LANES, (j + 1) * LANES)
            xs[t * rows : (t + 1) * rows, cut] = tl[t, :, cut] * sign

    def chunk_of(k):
        return lax.rem(my_chunk + nchunk // 2 + alternating(k) + nchunk, nchunk)

    low_bits = (tile_width - 1).bit_length()
    blocks_of_chunk = chunk // LANES
    fetches[3].wait()

    def build(k, hop):
        ch = chunk_of(k)
        for i in range(blocks_of_chunk):
            low = samples[pl.ds(ch * blocks_of_chunk + i, 1), :] & (tile_width - 1)
            base = parity_sign(lax.broadcasted_iota(jnp.int32, (16, LANES), 0) & low).astype(BF16)
            group = [base]
            for bit in range(4, low_bits):
                sign = (1 - 2 * ((low >> bit) & 1)).astype(F32)
                sign = jnp.broadcast_to(sign, (16, LANES)).astype(BF16)
                group = group + [g * sign for g in group]
            for j, g in enumerate(group):
                hop[16 * j : 16 * j + 16, i * LANES : (i + 1) * LANES] = g

    def multiply(k, hop):
        ch = chunk_of(k)
        y = jnp.dot(xs[...], hop[...], preferred_element_type=F32)
        for i in range(blocks_of_chunk):
            high = samples[pl.ds(ch * blocks_of_chunk + i, 1), :] >> low_bits
            coef = parity_sign(codes & high)
            total = None
            for t in range(slots):
                term = y[t * rows : (t + 1) * rows, i * LANES : (i + 1) * LANES] * coef[t : t + 1, :]
                total = term if total is None else total + term
            for p in range(CORES):
                terms[k, p, :, i * LANES : (i + 1) * LANES] = total[p * part : (p + 1) * part]

    def to_sibling(k):
        remote(terms.at[k, 1 - core], terms2.at[k], a_send, a_recv.at[k], sibling).start()

    xfar = nchunk - XNEAR
    zfar = nchunk - ZNEAR

    def to_partner(k):
        wait_bytes(terms2.at[k], a_recv.at[k])
        total = terms[k, core] + terms2[k]
        for i in range(planes):
            left = total[:, 2 * i * LANES : (2 * i + 1) * LANES]
            right = total[:, (2 * i + 1) * LANES : (2 * i + 2) * LANES]
            halves[k, i] = jnp.where(h == 0, left, right)
            given = jnp.where(h == 0, right, left)
            if k < xfar:
                far[k, i] = given.astype(BF16)
            else:
                other[k - xfar, i] = given
        if k < xfar:
            remote(far.at[k], far2.at[k], x_send, x_recv.at[k], partner).start()
        else:
            remote(other.at[k - xfar], other2.at[k - xfar], y_send, x_recv.at[k], partner).start()

    build(0, hop0)

    def pair(j, _):
        k = 2 * j
        build(k + 1, hop1)
        multiply(k, hop0)
        build(lax.rem(k + 2, nchunk), hop0)
        multiply(k + 1, hop1)
        return 0

    lax.fori_loop(0, nchunk // 2, pair, 0)

    pl.semaphore_wait(barrier, nz - 1 + nrow * QUAD - 1)
    for k in range(nchunk):
        to_sibling(k)
    for k in range(nchunk):
        to_partner(k)

    side = lax.rem(z, planes)
    for k in range(nchunk):
        arrived = far2.at[k] if k < xfar else other2.at[k - xfar]
        wait_bytes(arrived, x_recv.at[k])
        for i in range(planes):
            total = halves[k, i] + arrived[i].astype(F32)
            device = (row, at(chunk_of(k) * planes + i, h, core))
            if k < zfar:
                csend[k, i] = total.astype(BF16)
                remote(csend.at[k, i], crecv.at[k, side], c_send, c_recv, device).start()
            elif k < nchunk - 1:
                nsend[k - zfar, i] = total
                slot = (k - zfar) * planes + side
                remote(nsend.at[k - zfar, i], nrecv.at[slot], n_send, n_recv, device).start()
            else:

                @pl.when(side == i)
                def _():
                    own[...] = total

                @pl.when(side != i)
                def _():
                    nsend[k - zfar, i] = total
                    slot = (ZNEAR - 1) * planes + lax.rem(side - i + planes, planes) - 1
                    remote(nsend.at[k - zfar, i], nrecv.at[slot], n_send, n_recv, device).start()

    wait_bytes(nrecv, n_recv)
    total = own[...]
    for i in range(ZNEAR * planes - 1):
        total = total + nrecv[i]
    wait_bytes(crecv, c_recv)
    for k in range(zfar):
        for i in range(planes):
            total = total + crecv[k, i].astype(F32)
    total = total * (1.0 / math.sqrt(width))
    ag[z] = total.astype(BF16)

    def spread(k, _):
        device = (row, at(lax.rem(z + far_first(k), nz), h, core))
        remote(ag.at[z], ag.at[z], g_send, g_recv.at[z], device).start()
        return 0

    lax.fori_loop(0, nz - 1, spread, 0)

    my_rows = pl.ds(pl.multiple_of(row * rows + core * part, part), part)

    def in_plane(k, _):
        mate = lax.rem(row * CORES + core + k, nrow * CORES)
        device = (lax.div(mate, CORES), at(z, h, lax.rem(mate, CORES)))
        remote(ag.at[z], sc.at[my_rows], s_send, s_recv, device).start()
        return 0

    lax.fori_loop(1, nrow * CORES, in_plane, 0)
    pltpu.make_async_copy(ag.at[z], sc.at[my_rows], s_recv).start()

    sk[0] = total
    swap_sketch = remote(sk.at[0], sk.at[1], k_send, k_recv, sibling)
    swap_sketch.start()

    my_cols = pl.ds(pl.multiple_of(h * LANES, LANES), LANES)

    def forward(k, _):
        p = lax.rem(my_chunk + alternating(k) + nrow, nrow)
        for i in range(planes):
            z2 = p * planes + i

            @pl.when(z2 != z)
            def _():
                wait_bytes(ag.at[z2], g_recv.at[z2])

            for h2 in range(CHIPS):
                here = jnp.logical_and(p == row, jnp.logical_and(h2 == h, i == core))

                @pl.when(here)
                def _():
                    pltpu.make_async_copy(ag.at[z2], sr.at[my_rows, my_cols], f_recv).start()

                @pl.when(jnp.logical_not(here))
                def _():
                    remote(
                        ag.at[z2], sr.at[my_rows, my_cols], f_send, f_recv, (p, at(z, h2, i))
                    ).start()

        return 0

    lax.fori_loop(0, nrow, forward, 0)

    half = LANES // CORES
    swap_sketch.wait()
    for i in range(CORES):
        block = sk[jnp.where(core == i, 0, 1)]
        sketch_ref[i * part : (i + 1) * part, :] = jnp.where(core == 0, block[:, :half], block[:, half:])

    wait_bytes(sc, s_recv)
    wait_bytes(sr, f_recv)
    product = lax.dot_general(
        sc[...], sr[...], (((0,), (0,)), ((), ())), preferred_element_type=F32
    ) * (1.0 / (rows * nrow))
    gs[...] = jnp.where(core == 0, product[half:], product[:half])
    swap_product = remote(gs, gr, o_send, o_recv, sibling)
    swap_product.start()
    mine = jnp.where(core == 0, product[:half], product[half:])
    swap_product.wait()
    theirs = gr[...]
    cols = CHIPS * LANES
    gram_ref[:, :cols] = jnp.where(core == 0, mine, theirs)
    gram_ref[:, cols:] = jnp.where(core == 0, theirs, mine)

    wait_bytes(terms2, a_send)
    wait_bytes(far2, x_send)
    wait_bytes(other2, y_send)
    wait_bytes(crecv, c_send)
    wait_bytes(nrecv, n_send)
    wait_bytes(ag.at[pl.ds(0, nz - 1)], g_send)
    wait_bytes(sc.at[pl.ds(0, rows * nrow - part)], s_send)
    wait_bytes(sr.at[pl.ds(0, rows * nrow - part // CHIPS)], f_send)


def store(sketch_ref, gram_ref, sketch_hbm, gram_hbm, sems):
    copies = [
        pltpu.make_async_copy(src, dst, sems.at[i])
        for i, (src, dst) in enumerate([(gram_ref, gram_hbm), (sketch_ref, sketch_hbm)])
    ]
    for copy in copies:
        copy.start()
    for copy in copies:
        copy.wait()


def per_device(nrow, nz, tiles, block_cols, signs, samples):
    rows, slots, tile_width = tiles.shape
    width = samples.shape[0]
    part = rows // CORES
    half = LANES // CORES
    planes = nz // nrow
    chunk = planes * CHIPS * LANES
    nchunk = width // chunk
    dma = pltpu.SemaphoreType.DMA
    vmem = pl.BlockSpec(memory_space=pltpu.VMEM)
    hbm = pl.BlockSpec(memory_space=pltpu.HBM)
    sketch, gram_t = pl.pallas_call(
        functools.partial(kernel, nrow, nz),
        out_shape=(
            jax.ShapeDtypeStruct((rows, half), F32),
            jax.ShapeDtypeStruct((half, width // nrow), F32),
        ),
        in_specs=[hbm, hbm, hbm, hbm],
        out_specs=(vmem, vmem),
        scratch_shapes=[
            pltpu.VMEM((slots, rows, tile_width), BF16),
            pltpu.SMEM(block_cols.shape, jnp.int32),
            pltpu.VMEM((signs.shape[0] // LANES, LANES), jnp.int32),
            pltpu.VMEM((width // LANES, LANES), jnp.int32),
            pltpu.VMEM((slots * rows, tile_width), BF16),
            pltpu.VMEM((tile_width, chunk), BF16),
            pltpu.VMEM((tile_width, chunk), BF16),
            pltpu.VMEM((nchunk, CORES, part, chunk), F32),
            pltpu.VMEM((nchunk, part, chunk), F32),
            pltpu.VMEM((nchunk, planes, part, LANES), F32),
            pltpu.VMEM((XNEAR, planes, part, LANES), F32),
            pltpu.VMEM((XNEAR, planes, part, LANES), F32),
            pltpu.VMEM((nchunk - XNEAR, planes, part, LANES), BF16),
            pltpu.VMEM((nchunk - XNEAR, planes, part, LANES), BF16),
            pltpu.VMEM((part, LANES), F32),
            pltpu.VMEM((nchunk - ZNEAR, planes, part, LANES), BF16),
            pltpu.VMEM((nchunk - ZNEAR, planes, part, LANES), BF16),
            pltpu.VMEM((ZNEAR, planes, part, LANES), F32),
            pltpu.VMEM((ZNEAR * planes - 1, part, LANES), F32),
            pltpu.VMEM((nz, part, LANES), BF16),
            pltpu.VMEM((2, part, LANES), F32),
            pltpu.VMEM((rows * nrow, LANES), BF16),
            pltpu.VMEM((rows * nrow, CHIPS * LANES), BF16),
            pltpu.VMEM((half, CHIPS * LANES), F32),
            pltpu.VMEM((half, CHIPS * LANES), F32),
            dma((4,)),
            dma,
            dma((nchunk,)),
            dma,
            dma,
            dma((nchunk,)),
            dma,
            dma,
            dma,
            dma,
            dma,
            dma((nz,)),
            dma,
            dma,
            dma,
            dma,
            dma,
            dma,
            dma,
            dma,
        ],
        compiler_params=pltpu.CompilerParams(
            collective_id=0, has_side_effects=True, vmem_limit_bytes=32 << 20
        ),
    )(
        *(
            pltpu.with_memory_space_constraint(x, pltpu.HBM)
            for x in (
                tiles.transpose(1, 0, 2),
                block_cols,
                signs.reshape(-1, LANES),
                samples.reshape(-1, LANES),
            )
        )
    )
    sketch, gram_t = pl.pallas_call(
        store,
        out_shape=(
            jax.ShapeDtypeStruct(sketch.shape, F32),
            jax.ShapeDtypeStruct(gram_t.shape, F32),
        ),
        in_specs=[vmem, vmem],
        out_specs=(hbm, hbm),
        scratch_shapes=[dma((2,))],
    )(
        pltpu.with_memory_space_constraint(sketch, pltpu.VMEM),
        pltpu.with_memory_space_constraint(gram_t, pltpu.VMEM),
    )
    return sketch, gram_t.T


def solution(mesh):
    nrow = mesh.shape["row"]
    nz = mesh.shape["col"] // QUAD
    return jax.shard_map(
        functools.partial(per_device, nrow, nz),
        mesh=mesh,
        in_specs=(P("row", "col", None), P("row", "col"), P("col"), P()),
        out_specs=(P("row", "col"), P("row", "col")),
        check_vma=False,
    )
```

```python
import functools
import math

import jax
import jax.numpy as jnp
from jax import lax
from jax.experimental import pallas as pl
from jax.experimental.pallas import tpu as pltpu
from jax.sharding import PartitionSpec as P

MESH = pl.DeviceIdType.MESH
CHIPS = 2
CORES = 2
QUAD = CHIPS * CORES
LANES = 128
XNEAR = 5
ZNEAR = 1
F32 = jnp.float32
BF16 = jnp.bfloat16


def parity_sign(bits):
    for shift in (8, 4, 2, 1):
        bits = bits ^ (bits >> shift)
    return (1 - 2 * (bits & 1)).astype(F32)


def alternating(k):
    return lax.div(k + 1, 2) * (1 - 2 * lax.rem(k, 2))


def remote(src, dst, send_sem, recv_sem, device):
    return pltpu.make_async_remote_copy(
        src_ref=src,
        dst_ref=dst,
        send_sem=send_sem,
        recv_sem=recv_sem,
        device_id=device,
        device_id_type=MESH,
    )


def wait_bytes(ref, sem):
    pltpu.make_async_copy(ref, ref, sem).wait()


def kernel(
    nrow,
    nz,
    tiles_hbm,
    block_hbm,
    signs_hbm,
    samples_hbm,
    sketch_ref,
    gram_ref,
    tl,
    blocks,
    signs,
    samples,
    xs,
    hop0,
    hop1,
    terms,
    terms2,
    halves,
    other,
    other2,
    far,
    far2,
    own,
    csend,
    crecv,
    nsend,
    nrecv,
    ag,
    sk,
    sc,
    sr,
    gs,
    gr,
    in_sem,
    a_send,
    a_recv,
    x_send,
    y_send,
    x_recv,
    c_send,
    c_recv,
    n_send,
    n_recv,
    g_send,
    g_recv,
    k_send,
    k_recv,
    s_send,
    s_recv,
    w_send,
    w_recv,
    f_send,
    f_recv,
    o_send,
    o_recv,
):
    slots, rows, tile_width = tl.shape
    part = rows // CORES
    width = samples.shape[0] * LANES
    planes = nz // nrow
    chunk = planes * CHIPS * LANES
    nchunk = width // chunk
    row = lax.axis_index("row")
    col = lax.axis_index("col")
    z = lax.div(col, QUAD)
    q = lax.rem(col, QUAD)
    h = lax.div(q, CORES)
    core = lax.rem(q, CORES)
    my_chunk = lax.div(z, planes)
    sibling = (row, col + 1 - 2 * core)
    partner = (row, col + CORES * (1 - 2 * h))

    def at(z2, h2, core2):
        return z2 * QUAD + h2 * CORES + core2

    def far_first(k):
        return nz // 2 + alternating(k)

    fetches = [
        pltpu.make_async_copy(src, dst, in_sem.at[i])
        for i, (src, dst) in enumerate(
            [(block_hbm, blocks), (signs_hbm, signs), (tiles_hbm, tl), (samples_hbm, samples)]
        )
    ]
    for fetch in fetches:
        fetch.start()

    barrier = pltpu.get_barrier_semaphore()

    def greet_plane(k, _):
        mate = lax.rem(row * QUAD + q + k, nrow * QUAD)
        device = (lax.div(mate, QUAD), z * QUAD + lax.rem(mate, QUAD))
        pl.semaphore_signal(barrier, inc=1, device_id=device, device_id_type=MESH)
        return 0

    def greet_line(k, _):
        device = (row, at(lax.rem(z + far_first(k), nz), h, core))
        pl.semaphore_signal(barrier, inc=1, device_id=device, device_id_type=MESH)
        return 0

    lax.fori_loop(0, nz - 1, greet_line, 0)
    lax.fori_loop(1, nrow * QUAD, greet_plane, 0)

    per_block = tile_width // LANES
    where_row = lax.broadcasted_iota(jnp.int32, (8, LANES), 0)
    codes = jnp.zeros((8, LANES), jnp.int32)
    for fetch in fetches[:3]:
        fetch.wait()
    for t in range(slots):
        block = blocks[0, t]
        codes = jnp.where(where_row == t, col * (signs.shape[0] // per_block) + block, codes)
        for j in range(per_block):
            sign = signs[pl.ds(block * per_block + j, 1), :].astype(F32)
            sign = jnp.broadcast_to(sign, (rows, LANES)).astype(BF16)
            cut = slice(j * LANES, (j + 1) * LANES)
            xs[t * rows : (t + 1) * rows, cut] = tl[t, :, cut] * sign

    def chunk_of(k):
        return lax.rem(my_chunk + nchunk // 2 + alternating(k) + nchunk, nchunk)

    low_bits = (tile_width - 1).bit_length()
    blocks_of_chunk = chunk // LANES
    fetches[3].wait()

    def build(k, hop):
        ch = chunk_of(k)
        for i in range(blocks_of_chunk):
            low = samples[pl.ds(ch * blocks_of_chunk + i, 1), :] & (tile_width - 1)
            base = parity_sign(lax.broadcasted_iota(jnp.int32, (16, LANES), 0) & low).astype(BF16)
            group = [base]
            for bit in range(4, low_bits):
                sign = (1 - 2 * ((low >> bit) & 1)).astype(F32)
                sign = jnp.broadcast_to(sign, (16, LANES)).astype(BF16)
                group = group + [g * sign for g in group]
            for j, g in enumerate(group):
                hop[16 * j : 16 * j + 16, i * LANES : (i + 1) * LANES] = g

    def multiply(k, hop):
        ch = chunk_of(k)
        y = jnp.dot(xs[...], hop[...], preferred_element_type=F32)
        for i in range(blocks_of_chunk):
            high = samples[pl.ds(ch * blocks_of_chunk + i, 1), :] >> low_bits
            coef = parity_sign(codes & high)
            total = None
            for t in range(slots):
                term = y[t * rows : (t + 1) * rows, i * LANES : (i + 1) * LANES] * coef[t : t + 1, :]
                total = term if total is None else total + term
            for p in range(CORES):
                terms[k, p, :, i * LANES : (i + 1) * LANES] = total[p * part : (p + 1) * part]

    def to_sibling(k):
        remote(terms.at[k, 1 - core], terms2.at[k], a_send, a_recv.at[k], sibling).start()

    xfar = nchunk - XNEAR
    zfar = nchunk - ZNEAR

    def to_partner(k):
        wait_bytes(terms2.at[k], a_recv.at[k])
        total = terms[k, core] + terms2[k]
        for i in range(planes):
            left = total[:, 2 * i * LANES : (2 * i + 1) * LANES]
            right = total[:, (2 * i + 1) * LANES : (2 * i + 2) * LANES]
            halves[k, i] = jnp.where(h == 0, left, right)
            given = jnp.where(h == 0, right, left)
            if k < xfar:
                far[k, i] = given.astype(BF16)
            else:
                other[k - xfar, i] = given
        if k < xfar:
            remote(far.at[k], far2.at[k], x_send, x_recv.at[k], partner).start()
        else:
            remote(other.at[k - xfar], other2.at[k - xfar], y_send, x_recv.at[k], partner).start()

    build(0, hop0)

    def pair(j, _):
        k = 2 * j
        build(k + 1, hop1)
        multiply(k, hop0)
        build(lax.rem(k + 2, nchunk), hop0)
        multiply(k + 1, hop1)
        return 0

    lax.fori_loop(0, nchunk // 2, pair, 0)

    pl.semaphore_wait(barrier, nz - 1 + nrow * QUAD - 1)
    for k in range(nchunk):
        to_sibling(k)
    for k in range(nchunk):
        to_partner(k)

    side = lax.rem(z, planes)
    for k in range(nchunk):
        arrived = far2.at[k] if k < xfar else other2.at[k - xfar]
        wait_bytes(arrived, x_recv.at[k])
        for i in range(planes):
            total = halves[k, i] + arrived[i].astype(F32)
            device = (row, at(chunk_of(k) * planes + i, h, core))
            if k < zfar:
                csend[k, i] = total.astype(BF16)
                remote(csend.at[k, i], crecv.at[k, side], c_send, c_recv, device).start()
            elif k < nchunk - 1:
                nsend[k - zfar, i] = total
                slot = (k - zfar) * planes + side
                remote(nsend.at[k - zfar, i], nrecv.at[slot], n_send, n_recv, device).start()
            else:

                @pl.when(side == i)
                def _():
                    own[...] = total

                @pl.when(side != i)
                def _():
                    nsend[k - zfar, i] = total
                    slot = (ZNEAR - 1) * planes + lax.rem(side - i + planes, planes) - 1
                    remote(nsend.at[k - zfar, i], nrecv.at[slot], n_send, n_recv, device).start()

    wait_bytes(nrecv, n_recv)
    total = own[...]
    for i in range(ZNEAR * planes - 1):
        total = total + nrecv[i]
    wait_bytes(crecv, c_recv)
    for k in range(zfar):
        for i in range(planes):
            total = total + crecv[k, i].astype(F32)
    total = total * (1.0 / math.sqrt(width))
    ag[z] = total.astype(BF16)

    def spread(k, _):
        device = (row, at(lax.rem(z + far_first(k), nz), h, core))
        remote(ag.at[z], ag.at[z], g_send, g_recv.at[z], device).start()
        return 0

    lax.fori_loop(0, nz - 1, spread, 0)

    my_rows = pl.ds(pl.multiple_of(row * rows + core * part, part), part)

    def in_plane(k, _):
        device = (lax.rem(row + k, nrow), col)
        remote(ag.at[z], sc.at[row, core], s_send, s_recv, device).start()
        return 0

    lax.fori_loop(1, nrow, in_plane, 0)
    pltpu.make_async_copy(ag.at[z], sc.at[row, core], s_recv).start()

    sk[0] = total
    swap_sketch = remote(sk.at[0], sk.at[1], k_send, k_recv, sibling)
    swap_sketch.start()

    my_cols = pl.ds(pl.multiple_of(h * LANES, LANES), LANES)

    def forward(k, _):
        p = lax.rem(my_chunk + alternating(k) + nrow, nrow)
        for i in range(planes):
            z2 = p * planes + i

            @pl.when(z2 != z)
            def _():
                wait_bytes(ag.at[z2], g_recv.at[z2])

            for h2 in range(CHIPS):
                here = jnp.logical_and(p == row, jnp.logical_and(h2 == h, i == core))

                @pl.when(here)
                def _():
                    pltpu.make_async_copy(ag.at[z2], sr.at[my_rows, my_cols], f_recv).start()

                @pl.when(jnp.logical_not(here))
                def _():
                    remote(
                        ag.at[z2], sr.at[my_rows, my_cols], f_send, f_recv, (p, at(z, h2, i))
                    ).start()

        return 0

    lax.fori_loop(0, nrow, forward, 0)

    wait_bytes(sc.at[:, core], s_recv)
    swap_columns = remote(sc.at[:, core], sc.at[:, core], w_send, w_recv, sibling)
    swap_columns.start()

    half = LANES // CORES
    swap_sketch.wait()
    for i in range(CORES):
        block = sk[jnp.where(core == i, 0, 1)]
        sketch_ref[i * part : (i + 1) * part, :] = jnp.where(core == 0, block[:, :half], block[:, half:])

    swap_columns.wait()
    wait_bytes(sr, f_recv)
    product = lax.dot_general(
        sc[...].reshape(rows * nrow, LANES), sr[...], (((0,), (0,)), ((), ())), preferred_element_type=F32
    ) * (1.0 / (rows * nrow))
    gs[...] = jnp.where(core == 0, product[half:], product[:half])
    swap_product = remote(gs, gr, o_send, o_recv, sibling)
    swap_product.start()
    mine = jnp.where(core == 0, product[:half], product[half:])
    swap_product.wait()
    theirs = gr[...]
    cols = CHIPS * LANES
    gram_ref[:, :cols] = jnp.where(core == 0, mine, theirs)
    gram_ref[:, cols:] = jnp.where(core == 0, theirs, mine)

    wait_bytes(terms2, a_send)
    wait_bytes(far2, x_send)
    wait_bytes(other2, y_send)
    wait_bytes(crecv, c_send)
    wait_bytes(nrecv, n_send)
    wait_bytes(ag.at[pl.ds(0, nz - 1)], g_send)
    wait_bytes(sc.at[pl.ds(0, nrow - 1), 0], s_send)
    wait_bytes(sr.at[pl.ds(0, rows * nrow - part // CHIPS)], f_send)


def store(sketch_ref, gram_ref, sketch_hbm, gram_hbm, sems):
    copies = [
        pltpu.make_async_copy(src, dst, sems.at[i])
        for i, (src, dst) in enumerate([(gram_ref, gram_hbm), (sketch_ref, sketch_hbm)])
    ]
    for copy in copies:
        copy.start()
    for copy in copies:
        copy.wait()


def per_device(nrow, nz, tiles, block_cols, signs, samples):
    rows, slots, tile_width = tiles.shape
    width = samples.shape[0]
    part = rows // CORES
    half = LANES // CORES
    planes = nz // nrow
    chunk = planes * CHIPS * LANES
    nchunk = width // chunk
    dma = pltpu.SemaphoreType.DMA
    vmem = pl.BlockSpec(memory_space=pltpu.VMEM)
    hbm = pl.BlockSpec(memory_space=pltpu.HBM)
    sketch, gram_t = pl.pallas_call(
        functools.partial(kernel, nrow, nz),
        out_shape=(
            jax.ShapeDtypeStruct((rows, half), F32),
            jax.ShapeDtypeStruct((half, width // nrow), F32),
        ),
        in_specs=[hbm, hbm, hbm, hbm],
        out_specs=(vmem, vmem),
        scratch_shapes=[
            pltpu.VMEM((slots, rows, tile_width), BF16),
            pltpu.SMEM(block_cols.shape, jnp.int32),
            pltpu.VMEM((signs.shape[0] // LANES, LANES), jnp.int32),
            pltpu.VMEM((width // LANES, LANES), jnp.int32),
            pltpu.VMEM((slots * rows, tile_width), BF16),
            pltpu.VMEM((tile_width, chunk), BF16),
            pltpu.VMEM((tile_width, chunk), BF16),
            pltpu.VMEM((nchunk, CORES, part, chunk), F32),
            pltpu.VMEM((nchunk, part, chunk), F32),
            pltpu.VMEM((nchunk, planes, part, LANES), F32),
            pltpu.VMEM((XNEAR, planes, part, LANES), F32),
            pltpu.VMEM((XNEAR, planes, part, LANES), F32),
            pltpu.VMEM((nchunk - XNEAR, planes, part, LANES), BF16),
            pltpu.VMEM((nchunk - XNEAR, planes, part, LANES), BF16),
            pltpu.VMEM((part, LANES), F32),
            pltpu.VMEM((nchunk - ZNEAR, planes, part, LANES), BF16),
            pltpu.VMEM((nchunk - ZNEAR, planes, part, LANES), BF16),
            pltpu.VMEM((ZNEAR, planes, part, LANES), F32),
            pltpu.VMEM((ZNEAR * planes - 1, part, LANES), F32),
            pltpu.VMEM((nz, part, LANES), BF16),
            pltpu.VMEM((2, part, LANES), F32),
            pltpu.VMEM((nrow, CORES, part, LANES), BF16),
            pltpu.VMEM((rows * nrow, CHIPS * LANES), BF16),
            pltpu.VMEM((half, CHIPS * LANES), F32),
            pltpu.VMEM((half, CHIPS * LANES), F32),
            dma((4,)),
            dma,
            dma((nchunk,)),
            dma,
            dma,
            dma((nchunk,)),
            dma,
            dma,
            dma,
            dma,
            dma,
            dma((nz,)),
            dma,
            dma,
            dma,
            dma,
            dma,
            dma,
            dma,
            dma,
            dma,
            dma,
        ],
        compiler_params=pltpu.CompilerParams(
            collective_id=0, has_side_effects=True, vmem_limit_bytes=32 << 20
        ),
    )(
        *(
            pltpu.with_memory_space_constraint(x, pltpu.HBM)
            for x in (
                tiles.transpose(1, 0, 2),
                block_cols,
                signs.reshape(-1, LANES),
                samples.reshape(-1, LANES),
            )
        )
    )
    sketch, gram_t = pl.pallas_call(
        store,
        out_shape=(
            jax.ShapeDtypeStruct(sketch.shape, F32),
            jax.ShapeDtypeStruct(gram_t.shape, F32),
        ),
        in_specs=[vmem, vmem],
        out_specs=(hbm, hbm),
        scratch_shapes=[dma((2,))],
    )(
        pltpu.with_memory_space_constraint(sketch, pltpu.VMEM),
        pltpu.with_memory_space_constraint(gram_t, pltpu.VMEM),
    )
    return sketch, gram_t.T


def solution(mesh):
    nrow = mesh.shape["row"]
    nz = mesh.shape["col"] // QUAD
    return jax.shard_map(
        functools.partial(per_device, nrow, nz),
        mesh=mesh,
        in_specs=(P("row", "col", None), P("row", "col"), P("col"), P()),
        out_specs=(P("row", "col"), P("row", "col")),
        check_vma=False,
    )
```

```python
import functools
import math

import jax
import jax.numpy as jnp
from jax import lax
from jax.experimental import pallas as pl
from jax.experimental.pallas import tpu as pltpu
from jax.sharding import PartitionSpec as P

MESH = pl.DeviceIdType.MESH
CHIPS = 2
CORES = 2
QUAD = CHIPS * CORES
LANES = 128
XNEAR = 5
ZNEAR = 1
F32 = jnp.float32
BF16 = jnp.bfloat16


def parity_sign(bits):
    for shift in (8, 4, 2, 1):
        bits = bits ^ (bits >> shift)
    return (1 - 2 * (bits & 1)).astype(F32)


def alternating(k):
    return lax.div(k + 1, 2) * (1 - 2 * lax.rem(k, 2))


def remote(src, dst, send_sem, recv_sem, device):
    return pltpu.make_async_remote_copy(
        src_ref=src,
        dst_ref=dst,
        send_sem=send_sem,
        recv_sem=recv_sem,
        device_id=device,
        device_id_type=MESH,
    )


def wait_bytes(ref, sem):
    pltpu.make_async_copy(ref, ref, sem).wait()


def kernel(
    nrow,
    nz,
    tiles_hbm,
    block_hbm,
    signs_hbm,
    samples_hbm,
    sketch_ref,
    gram_ref,
    tl,
    blocks,
    signs,
    samples,
    xs,
    hop0,
    hop1,
    terms,
    terms2,
    halves,
    other,
    other2,
    far,
    far2,
    own,
    csend,
    crecv,
    nsend,
    nrecv,
    ag,
    sk,
    sc,
    sr,
    gs,
    gr,
    in_sem,
    a_send,
    a_recv,
    x_send,
    y_send,
    x_recv,
    c_send,
    c_recv,
    n_send,
    n_recv,
    g_send,
    g_recv,
    k_send,
    k_recv,
    s_send,
    s_recv,
    w_send,
    w_recv,
    f_send,
    f_recv,
    o_send,
    o_recv,
):
    slots, rows, tile_width = tl.shape
    part = rows // CORES
    width = samples.shape[0] * LANES
    planes = nz // nrow
    chunk = planes * CHIPS * LANES
    nchunk = width // chunk
    row = lax.axis_index("row")
    col = lax.axis_index("col")
    z = lax.div(col, QUAD)
    q = lax.rem(col, QUAD)
    h = lax.div(q, CORES)
    core = lax.rem(q, CORES)
    my_chunk = lax.div(z, planes)
    sibling = (row, col + 1 - 2 * core)
    partner = (row, col + CORES * (1 - 2 * h))

    def at(z2, h2, core2):
        return z2 * QUAD + h2 * CORES + core2

    def far_first(k):
        return nz // 2 + alternating(k)

    fetches = [
        pltpu.make_async_copy(src, dst, in_sem.at[i])
        for i, (src, dst) in enumerate(
            [(block_hbm, blocks), (signs_hbm, signs), (tiles_hbm, tl), (samples_hbm, samples)]
        )
    ]
    for fetch in fetches:
        fetch.start()

    barrier = pltpu.get_barrier_semaphore()

    def greet_plane(k, _):
        mate = lax.rem(row * QUAD + q + k, nrow * QUAD)
        device = (lax.div(mate, QUAD), z * QUAD + lax.rem(mate, QUAD))
        pl.semaphore_signal(barrier, inc=1, device_id=device, device_id_type=MESH)
        return 0

    def greet_line(k, _):
        device = (row, at(lax.rem(z + far_first(k), nz), h, core))
        pl.semaphore_signal(barrier, inc=1, device_id=device, device_id_type=MESH)
        return 0

    lax.fori_loop(0, nz - 1, greet_line, 0)
    lax.fori_loop(1, nrow * QUAD, greet_plane, 0)

    per_block = tile_width // LANES
    where_row = lax.broadcasted_iota(jnp.int32, (8, LANES), 0)
    codes = jnp.zeros((8, LANES), jnp.int32)
    for fetch in fetches[:3]:
        fetch.wait()
    for t in range(slots):
        block = blocks[0, t]
        codes = jnp.where(where_row == t, col * (signs.shape[0] // per_block) + block, codes)
        for j in range(per_block):
            sign = signs[pl.ds(block * per_block + j, 1), :].astype(F32)
            sign = jnp.broadcast_to(sign, (rows, LANES)).astype(BF16)
            cut = slice(j * LANES, (j + 1) * LANES)
            xs[t * rows : (t + 1) * rows, cut] = tl[t, :, cut] * sign

    def chunk_of(k):
        return lax.rem(my_chunk + nchunk // 2 + alternating(k) + nchunk, nchunk)

    low_bits = (tile_width - 1).bit_length()
    blocks_of_chunk = chunk // LANES
    fetches[3].wait()

    def build(k, hop):
        ch = chunk_of(k)
        for i in range(blocks_of_chunk):
            low = samples[pl.ds(ch * blocks_of_chunk + i, 1), :] & (tile_width - 1)
            base = parity_sign(lax.broadcasted_iota(jnp.int32, (16, LANES), 0) & low).astype(BF16)
            group = [base]
            for bit in range(4, low_bits):
                sign = (1 - 2 * ((low >> bit) & 1)).astype(F32)
                sign = jnp.broadcast_to(sign, (16, LANES)).astype(BF16)
                group = group + [g * sign for g in group]
            for j, g in enumerate(group):
                hop[16 * j : 16 * j + 16, i * LANES : (i + 1) * LANES] = g

    def multiply(k, hop):
        ch = chunk_of(k)
        y = jnp.dot(xs[...], hop[...], preferred_element_type=F32)
        for i in range(blocks_of_chunk):
            high = samples[pl.ds(ch * blocks_of_chunk + i, 1), :] >> low_bits
            coef = parity_sign(codes & high)
            total = None
            for t in range(slots):
                term = y[t * rows : (t + 1) * rows, i * LANES : (i + 1) * LANES] * coef[t : t + 1, :]
                total = term if total is None else total + term
            for p in range(CORES):
                terms[k, p, :, i * LANES : (i + 1) * LANES] = total[p * part : (p + 1) * part]

    def to_sibling(k):
        remote(terms.at[k, 1 - core], terms2.at[k], a_send, a_recv.at[k], sibling).start()

    xfar = nchunk - XNEAR
    zfar = nchunk - ZNEAR

    def to_partner(k):
        wait_bytes(terms2.at[k], a_recv.at[k])
        total = terms[k, core] + terms2[k]
        for i in range(planes):
            left = total[:, 2 * i * LANES : (2 * i + 1) * LANES]
            right = total[:, (2 * i + 1) * LANES : (2 * i + 2) * LANES]
            halves[k, i] = jnp.where(h == 0, left, right)
            given = jnp.where(h == 0, right, left)
            if k < xfar:
                far[k, i] = given.astype(BF16)
            else:
                other[k - xfar, i] = given
        if k < xfar:
            remote(far.at[k], far2.at[k], x_send, x_recv.at[k], partner).start()
        else:
            remote(other.at[k - xfar], other2.at[k - xfar], y_send, x_recv.at[k], partner).start()

    build(0, hop0)

    def pair(j, _):
        k = 2 * j
        build(k + 1, hop1)
        multiply(k, hop0)
        build(lax.rem(k + 2, nchunk), hop0)
        multiply(k + 1, hop1)
        return 0

    lax.fori_loop(0, nchunk // 2, pair, 0)

    pl.semaphore_wait(barrier, nz - 1 + nrow * QUAD - 1)
    for k in range(nchunk):
        to_sibling(k)
    for k in range(nchunk):
        to_partner(k)

    side = lax.rem(z, planes)
    for k in range(nchunk):
        arrived = far2.at[k] if k < xfar else other2.at[k - xfar]
        wait_bytes(arrived, x_recv.at[k])
        for i in range(planes):
            total = halves[k, i] + arrived[i].astype(F32)
            device = (row, at(chunk_of(k) * planes + i, h, core))
            if k < zfar:
                csend[k, i] = total.astype(BF16)
                remote(csend.at[k, i], crecv.at[k, side], c_send, c_recv, device).start()
            elif k < nchunk - 1:
                nsend[k - zfar, i] = total
                slot = (k - zfar) * planes + side
                remote(nsend.at[k - zfar, i], nrecv.at[slot], n_send, n_recv, device).start()
            else:

                @pl.when(side == i)
                def _():
                    own[...] = total

                @pl.when(side != i)
                def _():
                    nsend[k - zfar, i] = total
                    slot = (ZNEAR - 1) * planes + lax.rem(side - i + planes, planes) - 1
                    remote(nsend.at[k - zfar, i], nrecv.at[slot], n_send, n_recv, device).start()

    wait_bytes(nrecv, n_recv)
    total = own[...]
    for i in range(ZNEAR * planes - 1):
        total = total + nrecv[i]
    wait_bytes(crecv, c_recv)
    for k in range(zfar):
        for i in range(planes):
            total = total + crecv[k, i].astype(F32)
    total = total * (1.0 / math.sqrt(width))
    ag[z] = total.astype(BF16)

    def spread(k, _):
        device = (row, at(lax.rem(z + far_first(k), nz), h, core))
        remote(ag.at[z], ag.at[z], g_send, g_recv.at[z], device).start()
        return 0

    lax.fori_loop(0, nz - 1, spread, 0)

    my_rows = pl.ds(pl.multiple_of(row * rows + core * part, part), part)

    def in_plane(k, _):
        device = (lax.rem(row + k, nrow), col)
        remote(ag.at[z], sc.at[row, core], s_send, s_recv, device).start()
        return 0

    lax.fori_loop(1, nrow, in_plane, 0)
    pltpu.make_async_copy(ag.at[z], sc.at[row, core], s_recv).start()

    sk[0] = total
    swap_sketch = remote(sk.at[0], sk.at[1], k_send, k_recv, sibling)
    swap_sketch.start()

    my_cols = pl.ds(pl.multiple_of(h * LANES, LANES), LANES)
    for k in range(nz):
        offset = (k + 1) // 2 * (1 if k % 2 else -1)
        z2 = lax.rem(z - offset + nz, nz)
        if offset:
            wait_bytes(ag.at[z2], g_recv.at[z2])
        p = lax.div(z2, planes)
        i = lax.rem(z2, planes)
        for h2 in range(CHIPS):
            here = jnp.logical_and(p == row, jnp.logical_and(h2 == h, i == core))

            @pl.when(here)
            def _():
                pltpu.make_async_copy(ag.at[z2], sr.at[my_rows, my_cols], f_recv).start()

            @pl.when(jnp.logical_not(here))
            def _():
                device = (p, at(z, h2, i))
                remote(ag.at[z2], sr.at[my_rows, my_cols], f_send, f_recv, device).start()

    wait_bytes(sc.at[:, core], s_recv)
    swap_columns = remote(sc.at[:, core], sc.at[:, core], w_send, w_recv, sibling)
    swap_columns.start()

    half = LANES // CORES
    swap_sketch.wait()
    for i in range(CORES):
        block = sk[jnp.where(core == i, 0, 1)]
        sketch_ref[i * part : (i + 1) * part, :] = jnp.where(core == 0, block[:, :half], block[:, half:])

    swap_columns.wait()
    wait_bytes(sr, f_recv)
    product = lax.dot_general(
        sc[...].reshape(rows * nrow, LANES), sr[...], (((0,), (0,)), ((), ())), preferred_element_type=F32
    ) * (1.0 / (rows * nrow))
    gs[...] = jnp.where(core == 0, product[half:], product[:half])
    swap_product = remote(gs, gr, o_send, o_recv, sibling)
    swap_product.start()
    mine = jnp.where(core == 0, product[:half], product[half:])
    swap_product.wait()
    theirs = gr[...]
    cols = CHIPS * LANES
    gram_ref[:, :cols] = jnp.where(core == 0, mine, theirs)
    gram_ref[:, cols:] = jnp.where(core == 0, theirs, mine)

    wait_bytes(terms2, a_send)
    wait_bytes(far2, x_send)
    wait_bytes(other2, y_send)
    wait_bytes(crecv, c_send)
    wait_bytes(nrecv, n_send)
    wait_bytes(ag.at[pl.ds(0, nz - 1)], g_send)
    wait_bytes(sc.at[pl.ds(0, nrow - 1), 0], s_send)
    wait_bytes(sr.at[pl.ds(0, rows * nrow - part // CHIPS)], f_send)


def store(sketch_ref, gram_ref, sketch_hbm, gram_hbm, sems):
    copies = [
        pltpu.make_async_copy(src, dst, sems.at[i])
        for i, (src, dst) in enumerate([(gram_ref, gram_hbm), (sketch_ref, sketch_hbm)])
    ]
    for copy in copies:
        copy.start()
    for copy in copies:
        copy.wait()


def per_device(nrow, nz, tiles, block_cols, signs, samples):
    rows, slots, tile_width = tiles.shape
    width = samples.shape[0]
    part = rows // CORES
    half = LANES // CORES
    planes = nz // nrow
    chunk = planes * CHIPS * LANES
    nchunk = width // chunk
    dma = pltpu.SemaphoreType.DMA
    vmem = pl.BlockSpec(memory_space=pltpu.VMEM)
    hbm = pl.BlockSpec(memory_space=pltpu.HBM)
    sketch, gram_t = pl.pallas_call(
        functools.partial(kernel, nrow, nz),
        out_shape=(
            jax.ShapeDtypeStruct((rows, half), F32),
            jax.ShapeDtypeStruct((half, width // nrow), F32),
        ),
        in_specs=[hbm, hbm, hbm, hbm],
        out_specs=(vmem, vmem),
        scratch_shapes=[
            pltpu.VMEM((slots, rows, tile_width), BF16),
            pltpu.SMEM(block_cols.shape, jnp.int32),
            pltpu.VMEM((signs.shape[0] // LANES, LANES), jnp.int32),
            pltpu.VMEM((width // LANES, LANES), jnp.int32),
            pltpu.VMEM((slots * rows, tile_width), BF16),
            pltpu.VMEM((tile_width, chunk), BF16),
            pltpu.VMEM((tile_width, chunk), BF16),
            pltpu.VMEM((nchunk, CORES, part, chunk), F32),
            pltpu.VMEM((nchunk, part, chunk), F32),
            pltpu.VMEM((nchunk, planes, part, LANES), F32),
            pltpu.VMEM((XNEAR, planes, part, LANES), F32),
            pltpu.VMEM((XNEAR, planes, part, LANES), F32),
            pltpu.VMEM((nchunk - XNEAR, planes, part, LANES), BF16),
            pltpu.VMEM((nchunk - XNEAR, planes, part, LANES), BF16),
            pltpu.VMEM((part, LANES), F32),
            pltpu.VMEM((nchunk - ZNEAR, planes, part, LANES), BF16),
            pltpu.VMEM((nchunk - ZNEAR, planes, part, LANES), BF16),
            pltpu.VMEM((ZNEAR, planes, part, LANES), F32),
            pltpu.VMEM((ZNEAR * planes - 1, part, LANES), F32),
            pltpu.VMEM((nz, part, LANES), BF16),
            pltpu.VMEM((2, part, LANES), F32),
            pltpu.VMEM((nrow, CORES, part, LANES), BF16),
            pltpu.VMEM((rows * nrow, CHIPS * LANES), BF16),
            pltpu.VMEM((half, CHIPS * LANES), F32),
            pltpu.VMEM((half, CHIPS * LANES), F32),
            dma((4,)),
            dma,
            dma((nchunk,)),
            dma,
            dma,
            dma((nchunk,)),
            dma,
            dma,
            dma,
            dma,
            dma,
            dma((nz,)),
            dma,
            dma,
            dma,
            dma,
            dma,
            dma,
            dma,
            dma,
            dma,
            dma,
        ],
        compiler_params=pltpu.CompilerParams(
            collective_id=0, has_side_effects=True, vmem_limit_bytes=32 << 20
        ),
    )(
        *(
            pltpu.with_memory_space_constraint(x, pltpu.HBM)
            for x in (
                tiles.transpose(1, 0, 2),
                block_cols,
                signs.reshape(-1, LANES),
                samples.reshape(-1, LANES),
            )
        )
    )
    sketch, gram_t = pl.pallas_call(
        store,
        out_shape=(
            jax.ShapeDtypeStruct(sketch.shape, F32),
            jax.ShapeDtypeStruct(gram_t.shape, F32),
        ),
        in_specs=[vmem, vmem],
        out_specs=(hbm, hbm),
        scratch_shapes=[dma((2,))],
    )(
        pltpu.with_memory_space_constraint(sketch, pltpu.VMEM),
        pltpu.with_memory_space_constraint(gram_t, pltpu.VMEM),
    )
    return sketch, gram_t.T


def solution(mesh):
    nrow = mesh.shape["row"]
    nz = mesh.shape["col"] // QUAD
    return jax.shard_map(
        functools.partial(per_device, nrow, nz),
        mesh=mesh,
        in_specs=(P("row", "col", None), P("row", "col"), P("col"), P()),
        out_specs=(P("row", "col"), P("row", "col")),
        check_vma=False,
    )
```

```python
import functools
import math

import jax
import jax.numpy as jnp
from jax import lax
from jax.experimental import pallas as pl
from jax.experimental.pallas import tpu as pltpu
from jax.sharding import PartitionSpec as P

MESH = pl.DeviceIdType.MESH
CHIPS = 2
CORES = 2
QUAD = CHIPS * CORES
LANES = 128
XNEAR = 5
ZNEAR = 1
F32 = jnp.float32
BF16 = jnp.bfloat16


def parity_sign(bits):
    for shift in (8, 4, 2, 1):
        bits = bits ^ (bits >> shift)
    return (1 - 2 * (bits & 1)).astype(F32)


def alternating(k):
    return lax.div(k + 1, 2) * (1 - 2 * lax.rem(k, 2))


def remote(src, dst, send_sem, recv_sem, device):
    return pltpu.make_async_remote_copy(
        src_ref=src,
        dst_ref=dst,
        send_sem=send_sem,
        recv_sem=recv_sem,
        device_id=device,
        device_id_type=MESH,
    )


def wait_bytes(ref, sem):
    pltpu.make_async_copy(ref, ref, sem).wait()


def kernel(
    nrow,
    nz,
    tiles_hbm,
    block_hbm,
    signs_hbm,
    samples_hbm,
    sketch_ref,
    gram_ref,
    tl,
    blocks,
    signs,
    samples,
    xs,
    hop0,
    hop1,
    terms,
    terms2,
    halves,
    other,
    other2,
    far,
    far2,
    own,
    csend,
    crecv,
    nsend,
    nrecv,
    ag,
    sk,
    sc,
    sr,
    gs,
    gr,
    in_sem,
    a_send,
    a_recv,
    x_send,
    y_send,
    x_recv,
    c_send,
    c_recv,
    n_send,
    n_recv,
    g_send,
    g_recv,
    k_send,
    k_recv,
    s_send,
    s_recv,
    w_send,
    w_recv,
    f_send,
    f_recv,
    o_send,
    o_recv,
):
    slots, rows, tile_width = tl.shape
    part = rows // CORES
    width = samples.shape[0] * LANES
    planes = nz // nrow
    chunk = planes * CHIPS * LANES
    nchunk = width // chunk
    row = lax.axis_index("row")
    col = lax.axis_index("col")
    z = lax.div(col, QUAD)
    q = lax.rem(col, QUAD)
    h = lax.div(q, CORES)
    core = lax.rem(q, CORES)
    my_chunk = lax.div(z, planes)
    sibling = (row, col + 1 - 2 * core)
    partner = (row, col + CORES * (1 - 2 * h))

    def at(z2, h2, core2):
        return z2 * QUAD + h2 * CORES + core2

    def far_first(k):
        return nz // 2 + alternating(k)

    fetches = [
        pltpu.make_async_copy(src, dst, in_sem.at[i])
        for i, (src, dst) in enumerate(
            [(block_hbm, blocks), (signs_hbm, signs), (tiles_hbm, tl), (samples_hbm, samples)]
        )
    ]
    for fetch in fetches:
        fetch.start()

    barrier = pltpu.get_barrier_semaphore()

    def greet_plane(k, _):
        mate = lax.rem(row * QUAD + q + k, nrow * QUAD)
        device = (lax.div(mate, QUAD), z * QUAD + lax.rem(mate, QUAD))
        pl.semaphore_signal(barrier, inc=1, device_id=device, device_id_type=MESH)
        return 0

    def greet_line(k, _):
        device = (row, at(lax.rem(z + far_first(k), nz), h, core))
        pl.semaphore_signal(barrier, inc=1, device_id=device, device_id_type=MESH)
        return 0

    lax.fori_loop(0, nz - 1, greet_line, 0)
    lax.fori_loop(1, nrow * QUAD, greet_plane, 0)

    per_block = tile_width // LANES
    where_row = lax.broadcasted_iota(jnp.int32, (8, LANES), 0)
    codes = jnp.zeros((8, LANES), jnp.int32)
    for fetch in fetches[:3]:
        fetch.wait()
    for t in range(slots):
        block = blocks[0, t]
        codes = jnp.where(where_row == t, col * (signs.shape[0] // per_block) + block, codes)
        for j in range(per_block):
            sign = signs[pl.ds(block * per_block + j, 1), :].astype(F32)
            sign = jnp.broadcast_to(sign, (rows, LANES)).astype(BF16)
            cut = slice(j * LANES, (j + 1) * LANES)
            xs[t * rows : (t + 1) * rows, cut] = tl[t, :, cut] * sign

    def chunk_of(k):
        return lax.rem(my_chunk + nchunk // 2 + alternating(k) + nchunk, nchunk)

    low_bits = (tile_width - 1).bit_length()
    blocks_of_chunk = chunk // LANES
    fetches[3].wait()

    def build(k, hop):
        ch = chunk_of(k)
        for i in range(blocks_of_chunk):
            low = samples[pl.ds(ch * blocks_of_chunk + i, 1), :] & (tile_width - 1)
            base = parity_sign(lax.broadcasted_iota(jnp.int32, (16, LANES), 0) & low).astype(BF16)
            group = [base]
            for bit in range(4, low_bits):
                sign = (1 - 2 * ((low >> bit) & 1)).astype(F32)
                sign = jnp.broadcast_to(sign, (16, LANES)).astype(BF16)
                group = group + [g * sign for g in group]
            for j, g in enumerate(group):
                hop[16 * j : 16 * j + 16, i * LANES : (i + 1) * LANES] = g

    def multiply(k, hop):
        ch = chunk_of(k)
        y = jnp.dot(xs[...], hop[...], preferred_element_type=F32)
        for i in range(blocks_of_chunk):
            high = samples[pl.ds(ch * blocks_of_chunk + i, 1), :] >> low_bits
            coef = parity_sign(codes & high)
            total = None
            for t in range(slots):
                term = y[t * rows : (t + 1) * rows, i * LANES : (i + 1) * LANES] * coef[t : t + 1, :]
                total = term if total is None else total + term
            for p in range(CORES):
                terms[k, p, :, i * LANES : (i + 1) * LANES] = total[p * part : (p + 1) * part]

    def to_sibling(k):
        remote(terms.at[k, 1 - core], terms2.at[k], a_send, a_recv.at[k], sibling).start()

    xfar = nchunk - XNEAR
    zfar = nchunk - ZNEAR

    def to_partner(k):
        wait_bytes(terms2.at[k], a_recv.at[k])
        total = terms[k, core] + terms2[k]
        for i in range(planes):
            left = total[:, 2 * i * LANES : (2 * i + 1) * LANES]
            right = total[:, (2 * i + 1) * LANES : (2 * i + 2) * LANES]
            halves[k, i] = jnp.where(h == 0, left, right)
            given = jnp.where(h == 0, right, left)
            if k < xfar:
                far[k, i] = given.astype(BF16)
            else:
                other[k - xfar, i] = given
        if k < xfar:
            remote(far.at[k], far2.at[k], x_send, x_recv.at[k], partner).start()
        else:
            remote(other.at[k - xfar], other2.at[k - xfar], y_send, x_recv.at[k], partner).start()

    build(0, hop0)

    def pair(j, _):
        k = 2 * j
        build(k + 1, hop1)
        multiply(k, hop0)
        build(lax.rem(k + 2, nchunk), hop0)
        multiply(k + 1, hop1)
        return 0

    lax.fori_loop(0, nchunk // 2, pair, 0)

    pl.semaphore_wait(barrier, nz - 1 + nrow * QUAD - 1)
    for k in range(nchunk):
        to_sibling(k)
    for k in range(nchunk):
        to_partner(k)

    side = lax.rem(z, planes)
    for k in range(nchunk):
        arrived = far2.at[k] if k < xfar else other2.at[k - xfar]
        wait_bytes(arrived, x_recv.at[k])
        for i in range(planes):
            total = halves[k, i] + arrived[i].astype(F32)
            device = (row, at(chunk_of(k) * planes + i, h, core))
            if k < zfar:
                csend[k, i] = total.astype(BF16)
                remote(csend.at[k, i], crecv.at[k, side], c_send, c_recv, device).start()
            elif k < nchunk - 1:
                nsend[k - zfar, i] = total
                slot = (k - zfar) * planes + side
                remote(nsend.at[k - zfar, i], nrecv.at[slot], n_send, n_recv, device).start()
            else:

                @pl.when(side == i)
                def _():
                    own[...] = total

                @pl.when(side != i)
                def _():
                    nsend[k - zfar, i] = total
                    slot = (ZNEAR - 1) * planes + lax.rem(side - i + planes, planes) - 1
                    remote(nsend.at[k - zfar, i], nrecv.at[slot], n_send, n_recv, device).start()

    wait_bytes(nrecv, n_recv)
    total = own[...]
    for i in range(ZNEAR * planes - 1):
        total = total + nrecv[i]
    wait_bytes(crecv, c_recv)
    for k in range(zfar):
        for i in range(planes):
            total = total + crecv[k, i].astype(F32)
    total = total * (1.0 / math.sqrt(width))
    ag[z] = total.astype(BF16)

    def spread(k, _):
        device = (row, at(lax.rem(z + far_first(k), nz), h, core))
        remote(ag.at[z], ag.at[z], g_send, g_recv.at[z], device).start()
        return 0

    lax.fori_loop(0, nz - 1, spread, 0)

    my_rows = pl.ds(pl.multiple_of(row * rows + core * part, part), part)

    def in_plane(k, _):
        device = (lax.rem(row + k, nrow), col)
        remote(ag.at[z], sc.at[row, core], s_send, s_recv, device).start()
        return 0

    lax.fori_loop(1, nrow, in_plane, 0)
    pltpu.make_async_copy(ag.at[z], sc.at[row, core], s_recv).start()

    sk[0] = total
    swap_sketch = remote(sk.at[0], sk.at[1], k_send, k_recv, sibling)
    swap_sketch.start()

    my_cols = pl.ds(pl.multiple_of(h * LANES, LANES), LANES)

    def forward(k, _):
        p = lax.rem(my_chunk + alternating(k) + nrow, nrow)
        for i in range(planes):
            z2 = p * planes + i

            @pl.when(z2 != z)
            def _():
                wait_bytes(ag.at[z2], g_recv.at[z2])

            for h2 in range(CHIPS):
                here = jnp.logical_and(p == row, jnp.logical_and(h2 == h, i == core))

                @pl.when(here)
                def _():
                    pltpu.make_async_copy(ag.at[z2], sr.at[my_rows, my_cols], f_recv).start()

                @pl.when(jnp.logical_not(here))
                def _():
                    remote(
                        ag.at[z2], sr.at[my_rows, my_cols], f_send, f_recv, (p, at(z, h2, i))
                    ).start()

        return 0

    lax.fori_loop(0, nrow, forward, 0)

    wait_bytes(sc.at[:, core], s_recv)
    swap_columns = remote(sc.at[:, core], sc.at[:, core], w_send, w_recv, sibling)
    swap_columns.start()

    half = LANES // CORES
    swap_sketch.wait()
    for i in range(CORES):
        block = sk[jnp.where(core == i, 0, 1)]
        sketch_ref[i * part : (i + 1) * part, :] = jnp.where(core == 0, block[:, :half], block[:, half:])

    swap_columns.wait()
    wait_bytes(sr, f_recv)
    columns = sc[...].reshape(rows * nrow, LANES)
    low, high = columns[:, :half], columns[:, half:]

    def product(left):
        return lax.dot_general(
            left, sr[...], (((0,), (0,)), ((), ())), preferred_element_type=F32
        ) * (1.0 / (rows * nrow))

    gs[...] = product(jnp.where(core == 0, high, low))
    swap_product = remote(gs, gr, o_send, o_recv, sibling)
    swap_product.start()
    mine = product(jnp.where(core == 0, low, high))
    swap_product.wait()
    theirs = gr[...]
    cols = CHIPS * LANES
    gram_ref[:, :cols] = jnp.where(core == 0, mine, theirs)
    gram_ref[:, cols:] = jnp.where(core == 0, theirs, mine)

    wait_bytes(terms2, a_send)
    wait_bytes(far2, x_send)
    wait_bytes(other2, y_send)
    wait_bytes(crecv, c_send)
    wait_bytes(nrecv, n_send)
    wait_bytes(ag.at[pl.ds(0, nz - 1)], g_send)
    wait_bytes(sc.at[pl.ds(0, nrow - 1), 0], s_send)
    wait_bytes(sr.at[pl.ds(0, rows * nrow - part // CHIPS)], f_send)


def store(sketch_ref, gram_ref, sketch_hbm, gram_hbm, sems):
    copies = [
        pltpu.make_async_copy(src, dst, sems.at[i])
        for i, (src, dst) in enumerate([(gram_ref, gram_hbm), (sketch_ref, sketch_hbm)])
    ]
    for copy in copies:
        copy.start()
    for copy in copies:
        copy.wait()


def per_device(nrow, nz, tiles, block_cols, signs, samples):
    rows, slots, tile_width = tiles.shape
    width = samples.shape[0]
    part = rows // CORES
    half = LANES // CORES
    planes = nz // nrow
    chunk = planes * CHIPS * LANES
    nchunk = width // chunk
    dma = pltpu.SemaphoreType.DMA
    vmem = pl.BlockSpec(memory_space=pltpu.VMEM)
    hbm = pl.BlockSpec(memory_space=pltpu.HBM)
    sketch, gram_t = pl.pallas_call(
        functools.partial(kernel, nrow, nz),
        out_shape=(
            jax.ShapeDtypeStruct((rows, half), F32),
            jax.ShapeDtypeStruct((half, width // nrow), F32),
        ),
        in_specs=[hbm, hbm, hbm, hbm],
        out_specs=(vmem, vmem),
        scratch_shapes=[
            pltpu.VMEM((slots, rows, tile_width), BF16),
            pltpu.SMEM(block_cols.shape, jnp.int32),
            pltpu.VMEM((signs.shape[0] // LANES, LANES), jnp.int32),
            pltpu.VMEM((width // LANES, LANES), jnp.int32),
            pltpu.VMEM((slots * rows, tile_width), BF16),
            pltpu.VMEM((tile_width, chunk), BF16),
            pltpu.VMEM((tile_width, chunk), BF16),
            pltpu.VMEM((nchunk, CORES, part, chunk), F32),
            pltpu.VMEM((nchunk, part, chunk), F32),
            pltpu.VMEM((nchunk, planes, part, LANES), F32),
            pltpu.VMEM((XNEAR, planes, part, LANES), F32),
            pltpu.VMEM((XNEAR, planes, part, LANES), F32),
            pltpu.VMEM((nchunk - XNEAR, planes, part, LANES), BF16),
            pltpu.VMEM((nchunk - XNEAR, planes, part, LANES), BF16),
            pltpu.VMEM((part, LANES), F32),
            pltpu.VMEM((nchunk - ZNEAR, planes, part, LANES), BF16),
            pltpu.VMEM((nchunk - ZNEAR, planes, part, LANES), BF16),
            pltpu.VMEM((ZNEAR, planes, part, LANES), F32),
            pltpu.VMEM((ZNEAR * planes - 1, part, LANES), F32),
            pltpu.VMEM((nz, part, LANES), BF16),
            pltpu.VMEM((2, part, LANES), F32),
            pltpu.VMEM((nrow, CORES, part, LANES), BF16),
            pltpu.VMEM((rows * nrow, CHIPS * LANES), BF16),
            pltpu.VMEM((half, CHIPS * LANES), F32),
            pltpu.VMEM((half, CHIPS * LANES), F32),
            dma((4,)),
            dma,
            dma((nchunk,)),
            dma,
            dma,
            dma((nchunk,)),
            dma,
            dma,
            dma,
            dma,
            dma,
            dma((nz,)),
            dma,
            dma,
            dma,
            dma,
            dma,
            dma,
            dma,
            dma,
            dma,
            dma,
        ],
        compiler_params=pltpu.CompilerParams(
            collective_id=0, has_side_effects=True, vmem_limit_bytes=32 << 20
        ),
    )(
        *(
            pltpu.with_memory_space_constraint(x, pltpu.HBM)
            for x in (
                tiles.transpose(1, 0, 2),
                block_cols,
                signs.reshape(-1, LANES),
                samples.reshape(-1, LANES),
            )
        )
    )
    sketch, gram_t = pl.pallas_call(
        store,
        out_shape=(
            jax.ShapeDtypeStruct(sketch.shape, F32),
            jax.ShapeDtypeStruct(gram_t.shape, F32),
        ),
        in_specs=[vmem, vmem],
        out_specs=(hbm, hbm),
        scratch_shapes=[dma((2,))],
    )(
        pltpu.with_memory_space_constraint(sketch, pltpu.VMEM),
        pltpu.with_memory_space_constraint(gram_t, pltpu.VMEM),
    )
    return sketch, gram_t.T


def solution(mesh):
    nrow = mesh.shape["row"]
    nz = mesh.shape["col"] // QUAD
    return jax.shard_map(
        functools.partial(per_device, nrow, nz),
        mesh=mesh,
        in_specs=(P("row", "col", None), P("row", "col"), P("col"), P()),
        out_specs=(P("row", "col"), P("row", "col")),
        check_vma=False,
    )
```

```python
import functools
import math

import jax
import jax.numpy as jnp
from jax import lax
from jax.experimental import pallas as pl
from jax.experimental.pallas import tpu as pltpu
from jax.sharding import PartitionSpec as P

MESH = pl.DeviceIdType.MESH
CHIPS = 2
CORES = 2
QUAD = CHIPS * CORES
LANES = 128
XNEAR = 5
ZNEAR = 1
F32 = jnp.float32
BF16 = jnp.bfloat16


def parity_sign(bits):
    for shift in (8, 4, 2, 1):
        bits = bits ^ (bits >> shift)
    return (1 - 2 * (bits & 1)).astype(F32)


def alternating(k):
    return lax.div(k + 1, 2) * (1 - 2 * lax.rem(k, 2))


def remote(src, dst, send_sem, recv_sem, device):
    return pltpu.make_async_remote_copy(
        src_ref=src,
        dst_ref=dst,
        send_sem=send_sem,
        recv_sem=recv_sem,
        device_id=device,
        device_id_type=MESH,
    )


def wait_bytes(ref, sem):
    pltpu.make_async_copy(ref, ref, sem).wait()


def kernel(
    nrow,
    nz,
    tiles_hbm,
    block_hbm,
    signs_hbm,
    samples_hbm,
    sketch_ref,
    gram_ref,
    tl,
    blocks,
    signs,
    samples,
    xs,
    hop0,
    hop1,
    terms,
    terms2,
    halves,
    other,
    other2,
    far,
    far2,
    own,
    csend,
    crecv,
    nsend,
    nrecv,
    ag,
    sk,
    sc,
    sr,
    gs,
    gr,
    in_sem,
    a_send,
    a_recv,
    x_send,
    y_send,
    x_recv,
    c_send,
    c_recv,
    n_send,
    n_recv,
    g_send,
    g_recv,
    k_send,
    k_recv,
    s_send,
    s_recv,
    w_send,
    w_recv,
    f_send,
    f_recv,
    o_send,
    o_recv,
):
    slots, rows, tile_width = tl.shape
    part = rows // CORES
    width = samples.shape[0] * LANES
    planes = nz // nrow
    chunk = planes * CHIPS * LANES
    nchunk = width // chunk
    row = lax.axis_index("row")
    col = lax.axis_index("col")
    z = lax.div(col, QUAD)
    q = lax.rem(col, QUAD)
    h = lax.div(q, CORES)
    core = lax.rem(q, CORES)
    my_chunk = lax.div(z, planes)
    sibling = (row, col + 1 - 2 * core)
    partner = (row, col + CORES * (1 - 2 * h))

    def at(z2, h2, core2):
        return z2 * QUAD + h2 * CORES + core2

    def far_first(k):
        return nz // 2 + alternating(k)

    fetches = [
        pltpu.make_async_copy(src, dst, in_sem.at[i])
        for i, (src, dst) in enumerate(
            [(block_hbm, blocks), (signs_hbm, signs), (tiles_hbm, tl), (samples_hbm, samples)]
        )
    ]
    for fetch in fetches:
        fetch.start()

    barrier = pltpu.get_barrier_semaphore()

    def greet_plane(k, _):
        mate = lax.rem(row * QUAD + q + k, nrow * QUAD)
        device = (lax.div(mate, QUAD), z * QUAD + lax.rem(mate, QUAD))
        pl.semaphore_signal(barrier, inc=1, device_id=device, device_id_type=MESH)
        return 0

    def greet_line(k, _):
        device = (row, at(lax.rem(z + far_first(k), nz), h, core))
        pl.semaphore_signal(barrier, inc=1, device_id=device, device_id_type=MESH)
        return 0

    lax.fori_loop(0, nz - 1, greet_line, 0)
    lax.fori_loop(1, nrow * QUAD, greet_plane, 0)

    per_block = tile_width // LANES
    where_row = lax.broadcasted_iota(jnp.int32, (8, LANES), 0)
    codes = jnp.zeros((8, LANES), jnp.int32)
    for fetch in fetches[:3]:
        fetch.wait()
    for t in range(slots):
        block = blocks[0, t]
        codes = jnp.where(where_row == t, col * (signs.shape[0] // per_block) + block, codes)
        for j in range(per_block):
            sign = signs[pl.ds(block * per_block + j, 1), :].astype(F32)
            sign = jnp.broadcast_to(sign, (rows, LANES)).astype(BF16)
            cut = slice(j * LANES, (j + 1) * LANES)
            xs[t * rows : (t + 1) * rows, cut] = tl[t, :, cut] * sign

    def chunk_of(k):
        return lax.rem(my_chunk + nchunk // 2 + alternating(k) + nchunk, nchunk)

    low_bits = (tile_width - 1).bit_length()
    blocks_of_chunk = chunk // LANES
    fetches[3].wait()

    def build(k, hop):
        ch = chunk_of(k)
        for i in range(blocks_of_chunk):
            low = samples[pl.ds(ch * blocks_of_chunk + i, 1), :] & (tile_width - 1)
            base = parity_sign(lax.broadcasted_iota(jnp.int32, (16, LANES), 0) & low).astype(BF16)
            group = [base]
            for bit in range(4, low_bits):
                sign = (1 - 2 * ((low >> bit) & 1)).astype(F32)
                sign = jnp.broadcast_to(sign, (16, LANES)).astype(BF16)
                group = group + [g * sign for g in group]
            for j, g in enumerate(group):
                hop[16 * j : 16 * j + 16, i * LANES : (i + 1) * LANES] = g

    def multiply(k, hop):
        ch = chunk_of(k)
        y = jnp.dot(xs[...], hop[...], preferred_element_type=F32)
        for i in range(blocks_of_chunk):
            high = samples[pl.ds(ch * blocks_of_chunk + i, 1), :] >> low_bits
            coef = parity_sign(codes & high)
            total = None
            for t in range(slots):
                term = y[t * rows : (t + 1) * rows, i * LANES : (i + 1) * LANES] * coef[t : t + 1, :]
                total = term if total is None else total + term
            for p in range(CORES):
                terms[k, p, :, i * LANES : (i + 1) * LANES] = total[p * part : (p + 1) * part]

    def to_sibling(k):
        remote(terms.at[k, 1 - core], terms2.at[k], a_send, a_recv.at[k], sibling).start()

    xfar = nchunk - XNEAR
    zfar = nchunk - ZNEAR

    def to_partner(k):
        wait_bytes(terms2.at[k], a_recv.at[k])
        total = terms[k, core] + terms2[k]
        for i in range(planes):
            left = total[:, 2 * i * LANES : (2 * i + 1) * LANES]
            right = total[:, (2 * i + 1) * LANES : (2 * i + 2) * LANES]
            halves[k, i] = jnp.where(h == 0, left, right)
            given = jnp.where(h == 0, right, left)
            if k < xfar:
                far[k, i] = given.astype(BF16)
            else:
                other[k - xfar, i] = given
        if k < xfar:
            remote(far.at[k], far2.at[k], x_send, x_recv.at[k], partner).start()
        else:
            remote(other.at[k - xfar], other2.at[k - xfar], y_send, x_recv.at[k], partner).start()

    build(0, hop0)

    def pair(j, _):
        k = 2 * j
        build(k + 1, hop1)
        multiply(k, hop0)
        build(lax.rem(k + 2, nchunk), hop0)
        multiply(k + 1, hop1)
        return 0

    lax.fori_loop(0, nchunk // 2, pair, 0)

    pl.semaphore_wait(barrier, nz - 1 + nrow * QUAD - 1)
    for k in range(nchunk):
        to_sibling(k)
    for k in range(nchunk):
        to_partner(k)

    side = lax.rem(z, planes)
    for k in range(nchunk):
        arrived = far2.at[k] if k < xfar else other2.at[k - xfar]
        wait_bytes(arrived, x_recv.at[k])
        for i in range(planes):
            total = halves[k, i] + arrived[i].astype(F32)
            device = (row, at(chunk_of(k) * planes + i, h, core))
            if k < zfar:
                csend[k, i] = total.astype(BF16)
                remote(csend.at[k, i], crecv.at[k, side], c_send, c_recv, device).start()
            elif k < nchunk - 1:
                nsend[k - zfar, i] = total
                slot = (k - zfar) * planes + side
                remote(nsend.at[k - zfar, i], nrecv.at[slot], n_send, n_recv, device).start()
            else:

                @pl.when(side == i)
                def _():
                    own[...] = total

                @pl.when(side != i)
                def _():
                    nsend[k - zfar, i] = total
                    slot = (ZNEAR - 1) * planes + lax.rem(side - i + planes, planes) - 1
                    remote(nsend.at[k - zfar, i], nrecv.at[slot], n_send, n_recv, device).start()

    wait_bytes(nrecv, n_recv)
    total = own[...]
    for i in range(ZNEAR * planes - 1):
        total = total + nrecv[i]
    wait_bytes(crecv, c_recv)
    for k in range(zfar):
        for i in range(planes):
            total = total + crecv[k, i].astype(F32)
    total = total * (1.0 / math.sqrt(width))
    ag[z] = total.astype(BF16)

    def spread(k, _):
        device = (row, at(lax.rem(z + far_first(k), nz), h, core))
        remote(ag.at[z], ag.at[z], g_send, g_recv.at[z], device).start()
        return 0

    lax.fori_loop(0, nz - 1, spread, 0)

    my_rows = pl.ds(pl.multiple_of(row * rows + core * part, part), part)

    def in_plane(k, _):
        device = (lax.rem(row + k, nrow), col)
        remote(ag.at[z], sc.at[row, core], s_send, s_recv, device).start()
        return 0

    lax.fori_loop(1, nrow, in_plane, 0)
    pltpu.make_async_copy(ag.at[z], sc.at[row, core], s_recv).start()

    sk[0] = total
    swap_sketch = remote(sk.at[0], sk.at[1], k_send, k_recv, sibling)
    swap_sketch.start()

    def forward(k, _):
        p = lax.rem(my_chunk + alternating(k) + nrow, nrow)
        first = p * planes
        for i in range(planes):
            z2 = first + i

            @pl.when(z2 != z)
            def _():
                wait_bytes(ag.at[z2], g_recv.at[z2])

        src = ag.at[pl.ds(first, planes)]
        dst = sr.at[:, my_rows]
        for h2 in range(CHIPS):
            here = jnp.logical_and(p == row, jnp.logical_and(h2 == h, core == h))

            @pl.when(here)
            def _():
                pltpu.make_async_copy(src, dst, f_recv).start()

            @pl.when(jnp.logical_not(here))
            def _():
                remote(src, dst, f_send, f_recv, (p, at(z, h2, h))).start()

        return 0

    lax.fori_loop(0, nrow, forward, 0)

    wait_bytes(sc.at[:, core], s_recv)
    swap_columns = remote(sc.at[:, core], sc.at[:, core], w_send, w_recv, sibling)
    swap_columns.start()

    half = LANES // CORES
    swap_sketch.wait()
    for i in range(CORES):
        block = sk[jnp.where(core == i, 0, 1)]
        sketch_ref[i * part : (i + 1) * part, :] = jnp.where(core == 0, block[:, :half], block[:, half:])

    swap_columns.wait()
    wait_bytes(sr, f_recv)
    columns = sc[...].reshape(rows * nrow, LANES)
    product = jnp.concatenate(
        [
            lax.dot_general(columns, sr[i], (((0,), (0,)), ((), ())), preferred_element_type=F32)
            for i in range(planes)
        ],
        axis=1,
    ) * (1.0 / (rows * nrow))
    gs[...] = jnp.where(core == 0, product[half:], product[:half])
    swap_product = remote(gs, gr, o_send, o_recv, sibling)
    swap_product.start()
    mine = jnp.where(core == 0, product[:half], product[half:])
    swap_product.wait()
    theirs = gr[...]
    for i in range(planes):
        cut = slice(i * LANES, (i + 1) * LANES)
        left = 2 * i * LANES
        gram_ref[:, left : left + LANES] = jnp.where(core == 0, mine[:, cut], theirs[:, cut])
        gram_ref[:, left + LANES : left + 2 * LANES] = jnp.where(core == 0, theirs[:, cut], mine[:, cut])

    wait_bytes(terms2, a_send)
    wait_bytes(far2, x_send)
    wait_bytes(other2, y_send)
    wait_bytes(crecv, c_send)
    wait_bytes(nrecv, n_send)
    wait_bytes(ag.at[pl.ds(0, nz - 1)], g_send)
    wait_bytes(sc.at[pl.ds(0, nrow - 1), 0], s_send)

    @pl.when(core == h)
    def _():
        wait_bytes(sr.at[:, pl.ds(0, rows * nrow - part)], f_send)

    @pl.when(core != h)
    def _():
        wait_bytes(sr, f_send)


def store(sketch_ref, gram_ref, sketch_hbm, gram_hbm, sems):
    copies = [
        pltpu.make_async_copy(src, dst, sems.at[i])
        for i, (src, dst) in enumerate([(gram_ref, gram_hbm), (sketch_ref, sketch_hbm)])
    ]
    for copy in copies:
        copy.start()
    for copy in copies:
        copy.wait()


def per_device(nrow, nz, tiles, block_cols, signs, samples):
    rows, slots, tile_width = tiles.shape
    width = samples.shape[0]
    part = rows // CORES
    half = LANES // CORES
    planes = nz // nrow
    chunk = planes * CHIPS * LANES
    nchunk = width // chunk
    dma = pltpu.SemaphoreType.DMA
    vmem = pl.BlockSpec(memory_space=pltpu.VMEM)
    hbm = pl.BlockSpec(memory_space=pltpu.HBM)
    sketch, gram_t = pl.pallas_call(
        functools.partial(kernel, nrow, nz),
        out_shape=(
            jax.ShapeDtypeStruct((rows, half), F32),
            jax.ShapeDtypeStruct((half, width // nrow), F32),
        ),
        in_specs=[hbm, hbm, hbm, hbm],
        out_specs=(vmem, vmem),
        scratch_shapes=[
            pltpu.VMEM((slots, rows, tile_width), BF16),
            pltpu.SMEM(block_cols.shape, jnp.int32),
            pltpu.VMEM((signs.shape[0] // LANES, LANES), jnp.int32),
            pltpu.VMEM((width // LANES, LANES), jnp.int32),
            pltpu.VMEM((slots * rows, tile_width), BF16),
            pltpu.VMEM((tile_width, chunk), BF16),
            pltpu.VMEM((tile_width, chunk), BF16),
            pltpu.VMEM((nchunk, CORES, part, chunk), F32),
            pltpu.VMEM((nchunk, part, chunk), F32),
            pltpu.VMEM((nchunk, planes, part, LANES), F32),
            pltpu.VMEM((XNEAR, planes, part, LANES), F32),
            pltpu.VMEM((XNEAR, planes, part, LANES), F32),
            pltpu.VMEM((nchunk - XNEAR, planes, part, LANES), BF16),
            pltpu.VMEM((nchunk - XNEAR, planes, part, LANES), BF16),
            pltpu.VMEM((part, LANES), F32),
            pltpu.VMEM((nchunk - ZNEAR, planes, part, LANES), BF16),
            pltpu.VMEM((nchunk - ZNEAR, planes, part, LANES), BF16),
            pltpu.VMEM((ZNEAR, planes, part, LANES), F32),
            pltpu.VMEM((ZNEAR * planes - 1, part, LANES), F32),
            pltpu.VMEM((nz, part, LANES), BF16),
            pltpu.VMEM((2, part, LANES), F32),
            pltpu.VMEM((nrow, CORES, part, LANES), BF16),
            pltpu.VMEM((planes, rows * nrow, LANES), BF16),
            pltpu.VMEM((half, planes * LANES), F32),
            pltpu.VMEM((half, planes * LANES), F32),
            dma((4,)),
            dma,
            dma((nchunk,)),
            dma,
            dma,
            dma((nchunk,)),
            dma,
            dma,
            dma,
            dma,
            dma,
            dma((nz,)),
            dma,
            dma,
            dma,
            dma,
            dma,
            dma,
            dma,
            dma,
            dma,
            dma,
        ],
        compiler_params=pltpu.CompilerParams(
            collective_id=0, has_side_effects=True, vmem_limit_bytes=32 << 20
        ),
    )(
        *(
            pltpu.with_memory_space_constraint(x, pltpu.HBM)
            for x in (
                tiles.transpose(1, 0, 2),
                block_cols,
                signs.reshape(-1, LANES),
                samples.reshape(-1, LANES),
            )
        )
    )
    sketch, gram_t = pl.pallas_call(
        store,
        out_shape=(
            jax.ShapeDtypeStruct(sketch.shape, F32),
            jax.ShapeDtypeStruct(gram_t.shape, F32),
        ),
        in_specs=[vmem, vmem],
        out_specs=(hbm, hbm),
        scratch_shapes=[dma((2,))],
    )(
        pltpu.with_memory_space_constraint(sketch, pltpu.VMEM),
        pltpu.with_memory_space_constraint(gram_t, pltpu.VMEM),
    )
    return sketch, gram_t.T


def solution(mesh):
    nrow = mesh.shape["row"]
    nz = mesh.shape["col"] // QUAD
    return jax.shard_map(
        functools.partial(per_device, nrow, nz),
        mesh=mesh,
        in_specs=(P("row", "col", None), P("row", "col"), P("col"), P()),
        out_specs=(P("row", "col"), P("row", "col")),
        check_vma=False,
    )
```
